128 devices in a mesh: pair: 8 (over y_hi, x), mode: 16 (over y_lo, z, core).
Axes of the slice: x: 4, y: 4 (y_hi: 2, y_lo: 2; y = y_hi * 2 + y_lo), z: 4, core: 2. Of those that a mesh axis runs over, the one named last changes fastest.
Arguments:
- time_pairs: int32 [8, 2], P('pair'), may hold values from 0 to 7, as said below
- slot_of: int32 [8], replicated, may hold values from 0 to 7, each once
- elementals: bfloat16 [8, 4, 2, 1536, 1536], P('pair', None, None, 'mode'), may hold values from -0.109375 to 0.109375
- propagators: bfloat16 [8, 2, 1536, 1536], P('pair', None, 'mode'), may hold values from -6 to 6
Outputs:
- correlation: float32 [8, 4, 4, 2], P('pair')
- sink_block: bfloat16 [8, 4, 2, 1536, 1536], P('pair', None, None, 'mode')
The draws below stay inside these ranges and needn't reach their ends.
Inputs may be any that keep to these rules, and one draw needn't show every extreme that they name: `time_pairs`: the first column names each of the 8 timeslices once; in every row the second column differs from the first. `slot_of`: names every slot once; slot k of elementals lies on pair index k.
All inputs are finite; a program needn't handle non-finite values.
Results may differ from the reference program's by a relative error of at most 0.0051.
Values may be sent and summed in bfloat16 or wider, within the bound.
A program may use at most 128 MiB of HBM per device.

```python
import jax
import jax.numpy as jnp

OPS = 4
MAT = 1536
PAIRS = 8


def draw_time_pairs(key, part):
    key = jax.random.fold_in(key, 3)
    first_key, second_key = jax.random.split(key)
    first = jax.random.permutation(first_key, PAIRS).astype(jnp.int32)
    stride = jax.random.randint(second_key, (PAIRS,), 1, PAIRS).astype(jnp.int32)
    second = (first + stride) % PAIRS
    return jnp.stack([first, second], 1).astype(jnp.int32)


def block_scale(key, extent, cuts, least, top_value):
    def one(axis_at, parts):
        heights = jax.random.uniform(jax.random.fold_in(jax.random.fold_in(key, 6), axis_at), (parts,), jnp.float32, least / len(cuts), top_value / len(cuts))
        return jnp.repeat(jnp.exp(heights), extent[axis_at] // parts).reshape((-1,) + (1,) * (len(extent) - axis_at - 1))

    level = one(*cuts[0])
    for cut in cuts[1:]:
        level = level * one(*cut)
    return level


def noise(rng, extent, scale, limit, cuts=(), dtype=jnp.bfloat16):
    array = scale * jax.random.normal(rng, extent, jnp.float32)
    if cuts:
        array = array * block_scale(rng, extent, cuts, -0.22, 0.18)
    return jnp.clip(array, -limit, limit).astype(dtype)


def setup_inputs(seed: int = 0) -> dict:
    arg_keys = jax.random.split(jax.random.key(seed), 5)
    time_pairs = draw_time_pairs(jax.random.fold_in(arg_keys[4], 71), 0)
    slot_of = jax.random.permutation(arg_keys[1], PAIRS).astype(jnp.int32)
    elementals = noise(arg_keys[2], (PAIRS, OPS, 2, MAT, MAT), (2 * MAT) ** -0.5, 0.109375, ((0, 8), (3, 16)))
    propagators = noise(arg_keys[3], (PAIRS, 2, MAT, MAT), 1.0, 6.0, ((0, 8), (2, 16)))
    return {"time_pairs": time_pairs, "slot_of": slot_of, "elementals": elementals, "propagators": propagators}


def reference(time_pairs, slot_of, elementals, propagators):
    corr_list = []
    sink_list = []
    for pair_index in range(PAIRS):
        first_slot = slot_of[time_pairs[pair_index, 0]]
        second_slot = slot_of[time_pairs[pair_index, 1]]
        sink_ops = elementals[first_slot]
        source_ops = elementals[second_slot]
        prop_real = propagators[pair_index, 0]
        prop_imag = propagators[pair_index, 1]
        blocks = []
        adjoints = []
        for op_index in range(OPS):
            left_real = sink_ops[op_index, 0]
            left_imag = sink_ops[op_index, 1]
            sink_real = jnp.dot(left_real, prop_real, preferred_element_type=jnp.float32) - jnp.dot(left_imag, prop_imag, preferred_element_type=jnp.float32)
            sink_imag = jnp.dot(left_real, prop_imag, preferred_element_type=jnp.float32) + jnp.dot(left_imag, prop_real, preferred_element_type=jnp.float32)
            right_real = source_ops[op_index, 0].T
            right_imag = source_ops[op_index, 1].T
            adj_real = jnp.dot(prop_real, right_real, preferred_element_type=jnp.float32) + jnp.dot(prop_imag, right_imag, preferred_element_type=jnp.float32)
            adj_imag = jnp.dot(prop_imag, right_real, preferred_element_type=jnp.float32) - jnp.dot(prop_real, right_imag, preferred_element_type=jnp.float32)
            blocks.append(jnp.stack([sink_real, sink_imag]).astype(jnp.bfloat16))
            adjoints.append(jnp.stack([adj_real, adj_imag]).astype(jnp.bfloat16))
        block_stack = jnp.stack(blocks)
        adjoint_stack = jnp.stack(adjoints)
        block_wide = block_stack.astype(jnp.float32)
        adjoint_wide = adjoint_stack.astype(jnp.float32)
        real_part = jnp.einsum('gij,hij->gh', block_wide[:, 0], adjoint_wide[:, 0]) + jnp.einsum('gij,hij->gh', block_wide[:, 1], adjoint_wide[:, 1])
        imag_part = jnp.einsum('gij,hij->gh', block_wide[:, 1], adjoint_wide[:, 0]) - jnp.einsum('gij,hij->gh', block_wide[:, 0], adjoint_wide[:, 1])
        corr_list.append(jnp.stack([real_part, imag_part], -1) / MAT)
        sink_list.append(block_stack)
    return jnp.stack(corr_list), jnp.stack(sink_list)
```

```python
import jax
import jax.numpy as jnp
from jax import lax
from jax.experimental import pallas as pl
from jax.experimental.pallas import tpu as pltpu
from jax.sharding import PartitionSpec as P

MESH = pl.DeviceIdType.MESH
F32 = jnp.float32
BF16 = jnp.bfloat16
XS = 4
MODES = 16
OPS = 4
SLOTS = 8


def kernel(want_ref, elem, prop, sink_hbm, corr_ref,
           r0, r1, r2, r3, staged, w_sink, w_source, tau, stack, stack2, turned, arrived, sink,
           want_all, want_smem, parts,
           want_send, want_recv, p1_send, p1_recv, y_send, y_recv, p2_send, p2_recv,
           tau_send, tau_recv, t_send, t_recv, ps_send, ps_recv, local, out_sem):
    rows = elem.shape[2]
    order = elem.shape[3]
    quarter = order // XS
    gathered = (r0, r1, r2, r3)

    pair = lax.axis_index("pair")
    mode = lax.axis_index("mode")
    yh, x = pair // XS, pair % XS
    yl, z, core = mode // 8, (mode // 2) % 4, mode % 2

    def at_x(step):
        return (yh * XS + (x + step) % XS, mode)

    y_partner = ((1 - yh) * XS + x, mode)

    def chunk(y_at, z_at, core_at):
        return y_at * 8 + z_at * 2 + core_at

    def at_mode(y_at, z_at, core_at):
        return (pair, chunk(y_at, z_at, core_at))

    def remote(src, dst, send, recv, device):
        return pltpu.make_async_remote_copy(
            src_ref=src, dst_ref=dst, send_sem=send, recv_sem=recv,
            device_id=device, device_id_type=MESH)

    barrier = pltpu.get_barrier_semaphore()
    for step in range(1, XS):
        pl.semaphore_signal(barrier, inc=1, device_id=at_x(step), device_id_type=MESH)
    pl.semaphore_signal(barrier, inc=1, device_id=y_partner, device_id_type=MESH)

    @pl.loop(1, MODES)
    def _(step):
        pl.semaphore_signal(barrier, inc=1, device_id=(pair, (mode + step) % MODES), device_id_type=MESH)

    pl.semaphore_wait(barrier, XS - 1 + 1 + MODES - 1)

    want_copies = [
        remote(want_ref, want_all.at[x], want_send.at[s - 1], want_recv.at[s - 1], at_x(s))
        for s in range(1, XS)
    ]
    for copy in want_copies:
        copy.start()
    own_want = pltpu.make_async_copy(want_ref, want_all.at[x], local.at[0])
    own_want.start()

    def columns(at):
        return pl.ds(pl.multiple_of(at * quarter, 128), quarter)

    def stage1(o):
        copies = []
        for s in (2, 1, 3):
            copies.append(remote(
                elem.at[o, :, :, columns((x + s) % XS)], gathered[o].at[pair],
                p1_send.at[o, s - 1], p1_recv.at[o, s - 1], at_x(s)))
        own = pltpu.make_async_copy(elem.at[o, :, :, columns(x)], gathered[o].at[pair], local.at[1 + o])
        return copies, own

    first = [stage1(o) for o in range(OPS)]

    half = rows // 2
    tau_copies = {}

    def tau_rows(index, start=0, size=rows):
        return tau.at[:, pl.ds(pl.multiple_of(index * rows + start, 16), size), :]

    def pass_on(name, src, dst, device):
        k = len(tau_copies)
        copy = remote(src, dst, tau_send.at[k], tau_recv.at[k], device)
        copy.start()
        tau_copies[name] = copy

    def pass_rows(name, index, device, start=0, size=rows):
        ref = tau_rows(index, start, size)
        pass_on(name, ref, ref, device)

    zp, zm, zf = (z + 1) % 4, (z + 3) % 4, (z + 2) % 4
    up, down, sibling = at_mode(yl, zp, core), at_mode(yl, zm, core), at_mode(yl, z, 1 - core)
    own_chunk = chunk(yl, z, core)

    for copy in first[0][0]:
        copy.start()
    first[0][1].start()
    pass_on("y", prop, tau_rows(own_chunk), at_mode(1 - yl, z, core))
    pass_on("z+", prop, tau_rows(own_chunk), up)
    pass_on("z-", prop, tau_rows(own_chunk), down)
    pass_on("c", prop, tau_rows(own_chunk), sibling)
    own_tau = pltpu.make_async_copy(prop, tau_rows(own_chunk), local.at[1 + OPS])
    own_tau.start()
    for o in range(1, OPS):
        for copy in first[o][0]:
            copy.start()
        first[o][1].start()

    plane = pl.ds(yh * XS, XS)
    across = [
        remote(gathered[o].at[plane], gathered[o].at[plane], y_send.at[o], y_recv.at[o], y_partner)
        for o in range(OPS)
    ]

    def stage2(o):
        copies, own = first[o]
        own.wait()
        for copy in copies:
            copy.wait_recv()
        across[o].start()

    second = {}

    def stage3(o):
        across[o].wait_recv()
        for k, held in ((1, w_source), (0, w_sink)):
            for s in (2, 1, 3):
                slot = want_smem[(x + s) % XS, k, 0]
                staged[o, k, s - 1] = gathered[o][slot]
                copy = remote(
                    staged.at[o, k, s - 1], held.at[o, :, :, columns(x)],
                    p2_send.at[o, k, s - 1], p2_recv.at[o, k, s - 1], at_x(s))
                copy.start()
                second[o, k, s] = copy
            held[o, :, :, columns(x)] = gathered[o][want_smem[x, k, 0]]

    def wait_stage3(o, k):
        for s in range(1, XS):
            second[o, k, s].wait_recv()

    def relay(letter, y_at):
        tau_copies[letter + "z+"].wait_recv()
        below = chunk(y_at, zm, core)
        pass_rows(letter + "h+", below, up, 0, half)
        pass_rows(letter + "cz+", below, sibling)
        tau_copies[letter + "z-"].wait_recv()
        above = chunk(y_at, zp, core)
        pass_rows(letter + "h-", above, down, half, half)
        pass_rows(letter + "cz-", above, sibling)

    def relay_far(letter, y_at):
        far = chunk(y_at, zf, core)
        tau_copies[letter + "h+"].wait_recv()
        pass_rows(letter + "ch+", far, sibling, 0, half)
        tau_copies[letter + "h-"].wait_recv()
        pass_rows(letter + "ch-", far, sibling, half, half)

    stage2(0)
    own_want.wait()
    for copy in want_copies:
        copy.wait_recv()
    to_smem = pltpu.make_async_copy(want_all, want_smem, local.at[0])
    to_smem.start()
    stage2(1)
    tau_copies["y"].wait_recv()
    other = chunk(1 - yl, z, core)
    pass_rows("Vz+", other, up)
    pass_rows("Vz-", other, down)
    pass_rows("Vc", other, sibling)
    relay("", yl)
    stage2(2)
    to_smem.wait()
    stage3(0)
    relay_far("", yl)
    stage2(3)
    relay("V", 1 - yl)
    stage3(1)
    relay_far("V", 1 - yl)
    stage3(2)
    own_tau.wait()
    for name in ("c", "Vc", "cz+", "cz-", "Vcz+", "Vcz-", "ch+", "ch-", "Vch+", "Vch-"):
        tau_copies[name].wait_recv()

    span = 4 * rows
    dims = (((1,), (1,)), ((), ()))

    def source(h):
        for j in range(2):
            o = 2 * h + j
            wait_stage3(o, 1)
            real, imag = w_source[o, 0], w_source[o, 1]
            stack[pl.ds(2 * j * rows, rows), :] = real
            stack[pl.ds((2 * j + 1) * rows, rows), :] = -imag
            stack2[pl.ds(2 * j * rows, rows), :] = imag
            stack2[pl.ds((2 * j + 1) * rows, rows), :] = real

        @pl.loop(0, order // span)
        def _(i):
            at = pl.ds(pl.multiple_of(i * span, 16), span)
            total = lax.dot_general(tau[0, at, :], stack[...], dims, preferred_element_type=F32)
            total += lax.dot_general(tau[1, at, :], stack2[...], dims, preferred_element_type=F32)
            turned[h, pl.ds(i * 4, 4)] = total.astype(BF16).reshape(4, rows, span)

        @pl.loop(1, MODES)
        def _(step):
            to = (mode + step) % MODES
            remote(turned.at[h, to], arrived.at[h, mode],
                   t_send.at[h, step], t_recv.at[h, step], (pair, to)).start()

        pltpu.make_async_copy(turned.at[h, mode], arrived.at[h, mode], local.at[2 + OPS + h]).start()

    def wait_source(h):
        pltpu.make_async_copy(turned.at[h, mode], arrived.at[h, mode], local.at[2 + OPS + h]).wait()

        @pl.loop(1, MODES)
        def _(step):
            to = (mode + step) % MODES
            remote(turned.at[h, to], arrived.at[h, mode],
                   t_send.at[h, step], t_recv.at[h, step], (pair, to)).wait()

    wide = 256

    def sink_product(h):
        for j in range(2):
            o = 2 * h + j
            wait_stage3(o, 0)
            stack[pl.ds(2 * j * rows, rows), :] = -w_sink[o, 1]
            stack[pl.ds((2 * j + 1) * rows, rows), :] = w_sink[o, 0]

        @pl.loop(0, order // wide)
        def _(i):
            at = pl.ds(pl.multiple_of(i * wide, 128), wide)
            left = w_sink[2 * h:2 * h + 2].reshape(span, order)
            total = jnp.dot(left, tau[0, :, at], preferred_element_type=F32)
            total += jnp.dot(stack[...], tau[1, :, at], preferred_element_type=F32)
            sink[2 * h:2 * h + 2, :, :, at] = total.astype(BF16).reshape(2, 2, rows, wide)

        pltpu.make_async_copy(sink.at[pl.ds(2 * h, 2)], sink_hbm.at[pl.ds(2 * h, 2)], out_sem.at[h]).start()

    tall = 16

    def contract(h):
        group = lax.broadcasted_iota(jnp.int32, (tall, span), 1) // rows
        picks = [group == b for b in range(3)]

        def body(it, sums):
            sums = list(sums)
            row = pl.ds(pl.multiple_of((it // 4) * tall, tall), tall)
            g = it % 4
            blocks = [arrived[h, 4 * g + b, row, :].astype(F32) for b in range(4)]
            source_parts = []
            for a in range(4):
                moved = [
                    blocks[b] if a == b else pltpu.roll(blocks[b], (rows * (b - a)) % span, 1)
                    for b in range(4)
                ]
                source_parts.append(jnp.where(
                    picks[0], moved[0], jnp.where(picks[1], moved[1], jnp.where(picks[2], moved[2], moved[3]))))
            at = pl.ds(pl.multiple_of(g * span, 128), span)
            for o in range(OPS):
                s_re = sink[o, 0, row, at].astype(F32)
                s_im = sink[o, 1, row, at].astype(F32)
                for j in range(2):
                    t_re, t_im = source_parts[2 * j], source_parts[2 * j + 1]
                    for part, value in enumerate((s_re * t_re + s_im * t_im, s_im * t_re - s_re * t_im)):
                        value = value[:8] + value[8:]
                        value = value[:, :128] + value[:, 128:256] + value[:, 256:]
                        sums[(o * 2 + j) * 2 + part] += value
            return tuple(sums)

        zero = jnp.zeros((8, 128), F32)
        sums = lax.fori_loop(0, (rows // tall) * 4, body, (zero,) * (OPS * 4))
        for o in range(OPS):
            for j in range(2):
                for part in range(2):
                    index = (o * OPS + 2 * h + j) * 2 + part
                    parts[mode, pl.ds(index, 1), :] = jnp.sum(
                        sums[(o * 2 + j) * 2 + part], axis=0, keepdims=True)

    source(0)
    stage3(3)
    sink_product(0)
    source(1)
    sink_product(1)
    wait_source(0)
    contract(0)
    wait_source(1)
    contract(1)

    @pl.loop(1, MODES)
    def _(step):
        remote(parts.at[mode], parts.at[mode], ps_send.at[step], ps_recv.at[step],
               (pair, (mode + step) % MODES)).start()

    @pl.loop(1, MODES)
    def _(step):
        remote(parts.at[mode], parts.at[mode], ps_send.at[step], ps_recv.at[step],
               (pair, (mode + step) % MODES)).wait()

    total = parts[0]
    for n in range(1, MODES):
        total = total + parts[n]
    total = jnp.sum(total, axis=1, keepdims=True) * (1.0 / order)
    corr_ref[...] = jnp.broadcast_to(total, corr_ref.shape)

    for copy in want_copies:
        copy.wait_send()
    for copies, _ in first:
        for copy in copies:
            copy.wait_send()
    for copy in across:
        copy.wait_send()
    for copy in second.values():
        copy.wait_send()
    for copy in tau_copies.values():
        copy.wait_send()
    for h in range(2):
        pltpu.make_async_copy(sink.at[pl.ds(2 * h, 2)], sink_hbm.at[pl.ds(2 * h, 2)], out_sem.at[h]).wait()


def body(time_pairs, slot_of, elementals, propagators):
    _, ops, parts, rows, order = elementals.shape
    slots = slot_of.shape[0]
    positions = jnp.arange(slots, dtype=jnp.int32)
    wanted = jnp.sum(
        jnp.where(time_pairs.reshape(-1)[:, None] == positions[None, :], slot_of[None, :], 0), axis=1
    )
    line = lax.broadcasted_iota(jnp.int32, (8, 128), 0)
    want = jnp.where(line == 0, wanted[0], wanted[1]).astype(jnp.int32)
    quarter = order // XS
    dma = pltpu.SemaphoreType.DMA
    sink, corr = pl.pallas_call(
        kernel,
        out_shape=(
            jax.ShapeDtypeStruct((ops, 2, rows, order), BF16),
            jax.ShapeDtypeStruct((ops * ops * 2, 128), F32),
        ),
        in_specs=[
            pl.BlockSpec(memory_space=pltpu.VMEM),
            pl.BlockSpec(memory_space=pl.ANY),
            pl.BlockSpec(memory_space=pl.ANY),
        ],
        out_specs=(pl.BlockSpec(memory_space=pl.ANY), pl.BlockSpec(memory_space=pltpu.VMEM)),
        scratch_shapes=[
            *[pltpu.VMEM((slots, 2, rows, quarter), BF16)] * OPS,
            pltpu.VMEM((ops, 2, XS - 1, 2, rows, quarter), BF16),
            pltpu.VMEM((ops, 2, rows, order), BF16),
            pltpu.VMEM((ops, 2, rows, order), BF16),
            pltpu.VMEM((2, order, order), BF16),
            pltpu.VMEM((4 * rows, order), BF16),
            pltpu.VMEM((4 * rows, order), BF16),
            pltpu.VMEM((2, MODES, rows, 4 * rows), BF16),
            pltpu.VMEM((2, MODES, rows, 4 * rows), BF16),
            pltpu.VMEM((ops, 2, rows, order), BF16),
            pltpu.VMEM((XS, 8, 128), jnp.int32),
            pltpu.SMEM((XS, 8, 128), jnp.int32),
            pltpu.VMEM((MODES, ops * ops * 2, 128), F32),
            dma((XS - 1,)), dma((XS - 1,)),
            dma((OPS, XS - 1)), dma((OPS, XS - 1)),
            dma((OPS,)), dma((OPS,)),
            dma((OPS, 2, XS - 1)), dma((OPS, 2, XS - 1)),
            dma((24,)), dma((24,)),
            dma((2, MODES)), dma((2, MODES)),
            dma((MODES,)), dma((MODES,)),
            dma((2 + OPS + 2,)), dma((2,)),
        ],
        compiler_params=pltpu.CompilerParams(
            collective_id=0, has_side_effects=True, vmem_limit_bytes=56 << 20
        ),
        name="meson",
    )(want, elementals[0], propagators[0])
    return corr[:, 0].reshape(1, ops, ops, 2), sink[None]


def solution(mesh):
    in_specs = (
        P("pair", None),
        P(),
        P("pair", None, None, "mode", None),
        P("pair", None, "mode", None),
    )
    out_specs = (P("pair", None, None, None), P("pair", None, None, "mode", None))
    return jax.shard_map(body, mesh=mesh, in_specs=in_specs, out_specs=out_specs, check_vma=False)
```

```python
import jax
import jax.numpy as jnp
from jax import lax
from jax.experimental import pallas as pl
from jax.experimental.pallas import tpu as pltpu
from jax.sharding import PartitionSpec as P

MESH = pl.DeviceIdType.MESH
F32 = jnp.float32
BF16 = jnp.bfloat16
XS = 4
MODES = 16
OPS = 4
SLOTS = 8


def kernel(times, slots, elem_ref, prop_ref, sink_ref, corr_ref,
           r0, r1, r2, r3, staged, w_sink, w_source, tau, stack, stack2, turned, arrived, sink,
           want_all, want_smem, parts,
           want_send, want_recv, p1_send, p1_recv, y_send, y_recv, p2_send, p2_recv,
           tau_send, tau_recv, t_send, t_recv, ps_send, ps_recv, local, out_sem):
    elem, prop, sink_hbm = elem_ref.at[0], prop_ref.at[0], sink_ref.at[0]
    rows = elem.shape[2]
    order = elem.shape[3]
    quarter = order // XS
    gathered = (r0, r1, r2, r3)

    pair = lax.axis_index("pair")
    mode = lax.axis_index("mode")
    yh, x = pair // XS, pair % XS
    yl, z, core = mode // 8, (mode // 2) % 4, mode % 2

    def at_x(step):
        return (yh * XS + (x + step) % XS, mode)

    y_partner = ((1 - yh) * XS + x, mode)

    def chunk(y_at, z_at, core_at):
        return y_at * 8 + z_at * 2 + core_at

    def at_mode(y_at, z_at, core_at):
        return (pair, chunk(y_at, z_at, core_at))

    def remote(src, dst, send, recv, device):
        return pltpu.make_async_remote_copy(
            src_ref=src, dst_ref=dst, send_sem=send, recv_sem=recv,
            device_id=device, device_id_type=MESH)

    line = lax.broadcasted_iota(jnp.int32, (8, 128), 0)
    want_all[x] = jnp.where(line == 0, slots[times[0, 0]], slots[times[0, 1]])

    barrier = pltpu.get_barrier_semaphore()
    for step in range(1, XS):
        pl.semaphore_signal(barrier, inc=1, device_id=at_x(step), device_id_type=MESH)
    pl.semaphore_signal(barrier, inc=1, device_id=y_partner, device_id_type=MESH)

    @pl.loop(1, MODES)
    def _(step):
        pl.semaphore_signal(barrier, inc=1, device_id=(pair, (mode + step) % MODES), device_id_type=MESH)

    pl.semaphore_wait(barrier, XS - 1 + 1 + MODES - 1)

    want_copies = [
        remote(want_all.at[x], want_all.at[x], want_send.at[s - 1], want_recv.at[s - 1], at_x(s))
        for s in range(1, XS)
    ]
    for copy in want_copies:
        copy.start()

    def columns(at):
        return pl.ds(pl.multiple_of(at * quarter, 128), quarter)

    def stage1(o):
        copies = []
        for s in (2, 1, 3):
            copies.append(remote(
                elem.at[o, :, :, columns((x + s) % XS)], gathered[o].at[pair],
                p1_send.at[o, s - 1], p1_recv.at[o, s - 1], at_x(s)))
        own = pltpu.make_async_copy(elem.at[o, :, :, columns(x)], gathered[o].at[pair], local.at[1 + o])
        return copies, own

    first = [stage1(o) for o in range(OPS)]

    half = rows // 2
    tau_copies = {}

    def tau_rows(index, start=0, size=rows):
        return tau.at[:, pl.ds(pl.multiple_of(index * rows + start, 16), size), :]

    def pass_on(name, src, dst, device):
        k = len(tau_copies)
        copy = remote(src, dst, tau_send.at[k], tau_recv.at[k], device)
        copy.start()
        tau_copies[name] = copy

    def pass_rows(name, index, device, start=0, size=rows):
        ref = tau_rows(index, start, size)
        pass_on(name, ref, ref, device)

    zp, zm, zf = (z + 1) % 4, (z + 3) % 4, (z + 2) % 4
    up, down, sibling = at_mode(yl, zp, core), at_mode(yl, zm, core), at_mode(yl, z, 1 - core)
    own_chunk = chunk(yl, z, core)

    for copy in first[0][0]:
        copy.start()
    first[0][1].start()
    pass_on("y", prop, tau_rows(own_chunk), at_mode(1 - yl, z, core))
    pass_on("z+", prop, tau_rows(own_chunk), up)
    pass_on("z-", prop, tau_rows(own_chunk), down)
    pass_on("c", prop, tau_rows(own_chunk), sibling)
    own_tau = pltpu.make_async_copy(prop, tau_rows(own_chunk), local.at[1 + OPS])
    own_tau.start()
    for o in range(1, OPS):
        for copy in first[o][0]:
            copy.start()
        first[o][1].start()

    plane = pl.ds(yh * XS, XS)
    across = [
        remote(gathered[o].at[plane], gathered[o].at[plane], y_send.at[o], y_recv.at[o], y_partner)
        for o in range(OPS)
    ]

    def stage2(o):
        copies, own = first[o]
        own.wait()
        for copy in copies:
            copy.wait_recv()
        across[o].start()

    second = {}

    def stage3(o):
        across[o].wait_recv()
        for k, held in ((1, w_source), (0, w_sink)):
            for s in (2, 1, 3):
                slot = want_smem[(x + s) % XS, k, 0]
                staged[o, k, s - 1] = gathered[o][slot]
                copy = remote(
                    staged.at[o, k, s - 1], held.at[o, :, :, columns(x)],
                    p2_send.at[o, k, s - 1], p2_recv.at[o, k, s - 1], at_x(s))
                copy.start()
                second[o, k, s] = copy
            held[o, :, :, columns(x)] = gathered[o][want_smem[x, k, 0]]

    def wait_stage3(o, k):
        for s in range(1, XS):
            second[o, k, s].wait_recv()

    def relay(letter, y_at):
        tau_copies[letter + "z+"].wait_recv()
        below = chunk(y_at, zm, core)
        pass_rows(letter + "h+", below, up, 0, half)
        pass_rows(letter + "cz+", below, sibling)
        tau_copies[letter + "z-"].wait_recv()
        above = chunk(y_at, zp, core)
        pass_rows(letter + "h-", above, down, half, half)
        pass_rows(letter + "cz-", above, sibling)

    def relay_far(letter, y_at):
        far = chunk(y_at, zf, core)
        tau_copies[letter + "h+"].wait_recv()
        pass_rows(letter + "ch+", far, sibling, 0, half)
        tau_copies[letter + "h-"].wait_recv()
        pass_rows(letter + "ch-", far, sibling, half, half)

    stage2(0)
    for copy in want_copies:
        copy.wait_recv()
    to_smem = pltpu.make_async_copy(want_all, want_smem, local.at[0])
    to_smem.start()
    stage2(1)
    tau_copies["y"].wait_recv()
    other = chunk(1 - yl, z, core)
    pass_rows("Vz+", other, up)
    pass_rows("Vz-", other, down)
    pass_rows("Vc", other, sibling)
    relay("", yl)
    stage2(2)
    to_smem.wait()
    stage3(0)
    relay_far("", yl)
    stage2(3)
    relay("V", 1 - yl)
    stage3(1)
    relay_far("V", 1 - yl)
    stage3(2)
    own_tau.wait()
    for name in ("c", "Vc", "cz+", "cz-", "Vcz+", "Vcz-", "ch+", "ch-", "Vch+", "Vch-"):
        tau_copies[name].wait_recv()

    span = 4 * rows
    dims = (((1,), (1,)), ((), ()))

    def source(h):
        for j in range(2):
            o = 2 * h + j
            wait_stage3(o, 1)
            real, imag = w_source[o, 0], w_source[o, 1]
            stack[pl.ds(2 * j * rows, rows), :] = real
            stack[pl.ds((2 * j + 1) * rows, rows), :] = -imag
            stack2[pl.ds(2 * j * rows, rows), :] = imag
            stack2[pl.ds((2 * j + 1) * rows, rows), :] = real

        @pl.loop(0, order // span)
        def _(i):
            at = pl.ds(pl.multiple_of(i * span, 16), span)
            total = lax.dot_general(tau[0, at, :], stack[...], dims, preferred_element_type=F32)
            total += lax.dot_general(tau[1, at, :], stack2[...], dims, preferred_element_type=F32)
            turned[h, pl.ds(i * 4, 4)] = total.astype(BF16).reshape(4, rows, span)

        @pl.loop(1, MODES)
        def _(step):
            to = (mode + step) % MODES
            remote(turned.at[h, to], arrived.at[h, mode],
                   t_send.at[h, step], t_recv.at[h, step], (pair, to)).start()

        pltpu.make_async_copy(turned.at[h, mode], arrived.at[h, mode], local.at[2 + OPS + h]).start()

    def wait_source(h):
        pltpu.make_async_copy(turned.at[h, mode], arrived.at[h, mode], local.at[2 + OPS + h]).wait()

        @pl.loop(1, MODES)
        def _(step):
            to = (mode + step) % MODES
            remote(turned.at[h, to], arrived.at[h, mode],
                   t_send.at[h, step], t_recv.at[h, step], (pair, to)).wait()

    wide = 256

    def sink_product(h):
        for j in range(2):
            o = 2 * h + j
            wait_stage3(o, 0)
            stack[pl.ds(2 * j * rows, rows), :] = -w_sink[o, 1]
            stack[pl.ds((2 * j + 1) * rows, rows), :] = w_sink[o, 0]

        @pl.loop(0, order // wide)
        def _(i):
            at = pl.ds(pl.multiple_of(i * wide, 128), wide)
            left = w_sink[2 * h:2 * h + 2].reshape(span, order)
            total = jnp.dot(left, tau[0, :, at], preferred_element_type=F32)
            total += jnp.dot(stack[...], tau[1, :, at], preferred_element_type=F32)
            sink[2 * h:2 * h + 2, :, :, at] = total.astype(BF16).reshape(2, 2, rows, wide)

        pltpu.make_async_copy(sink.at[pl.ds(2 * h, 2)], sink_hbm.at[pl.ds(2 * h, 2)], out_sem.at[h]).start()

    tall = 16

    def contract(h):
        group = lax.broadcasted_iota(jnp.int32, (tall, span), 1) // rows
        picks = [group == b for b in range(3)]

        def body(it, sums):
            sums = list(sums)
            row = pl.ds(pl.multiple_of((it // 4) * tall, tall), tall)
            g = it % 4
            blocks = [arrived[h, 4 * g + b, row, :].astype(F32) for b in range(4)]
            source_parts = []
            for a in range(4):
                moved = [
                    blocks[b] if a == b else pltpu.roll(blocks[b], (rows * (b - a)) % span, 1)
                    for b in range(4)
                ]
                source_parts.append(jnp.where(
                    picks[0], moved[0], jnp.where(picks[1], moved[1], jnp.where(picks[2], moved[2], moved[3]))))
            at = pl.ds(pl.multiple_of(g * span, 128), span)
            for o in range(OPS):
                s_re = sink[o, 0, row, at].astype(F32)
                s_im = sink[o, 1, row, at].astype(F32)
                for j in range(2):
                    t_re, t_im = source_parts[2 * j], source_parts[2 * j + 1]
                    for part, value in enumerate((s_re * t_re + s_im * t_im, s_im * t_re - s_re * t_im)):
                        value = value[:8] + value[8:]
                        value = value[:, :128] + value[:, 128:256] + value[:, 256:]
                        sums[(o * 2 + j) * 2 + part] += value
            return tuple(sums)

        zero = jnp.zeros((8, 128), F32)
        sums = lax.fori_loop(0, (rows // tall) * 4, body, (zero,) * (OPS * 4))
        for o in range(OPS):
            for j in range(2):
                for part in range(2):
                    index = (o * 2 + part) * OPS + 2 * h + j
                    parts[mode, pl.ds(index, 1), :] = jnp.sum(
                        sums[(o * 2 + j) * 2 + part], axis=0, keepdims=True)

    source(0)
    stage3(3)
    sink_product(0)
    source(1)
    sink_product(1)
    wait_source(0)
    contract(0)
    wait_source(1)
    contract(1)

    @pl.loop(1, MODES)
    def _(step):
        remote(parts.at[mode], parts.at[mode], ps_send.at[step], ps_recv.at[step],
               (pair, (mode + step) % MODES)).start()

    @pl.loop(1, MODES)
    def _(step):
        remote(parts.at[mode], parts.at[mode], ps_send.at[step], ps_recv.at[step],
               (pair, (mode + step) % MODES)).wait()

    total = parts[0]
    for n in range(1, MODES):
        total = total + parts[n]
    total = jnp.sum(total, axis=1, keepdims=True) * (1.0 / order)
    total = jnp.broadcast_to(total, parts.shape[1:])
    lane = lax.broadcasted_iota(jnp.int32, (OPS, 2), 1)
    for o in range(OPS):
        at = 2 * OPS * o
        corr_ref[0, o] = jnp.where(lane == 0, total[at:at + OPS, :2], total[at + OPS:at + 2 * OPS, :2])

    for copy in want_copies:
        copy.wait_send()
    for copies, _ in first:
        for copy in copies:
            copy.wait_send()
    for copy in across:
        copy.wait_send()
    for copy in second.values():
        copy.wait_send()
    for copy in tau_copies.values():
        copy.wait_send()
    for h in range(2):
        pltpu.make_async_copy(sink.at[pl.ds(2 * h, 2)], sink_hbm.at[pl.ds(2 * h, 2)], out_sem.at[h]).wait()


def body(time_pairs, slot_of, elementals, propagators):
    _, ops, parts, rows, order = elementals.shape
    slots = slot_of.shape[0]
    quarter = order // XS
    dma = pltpu.SemaphoreType.DMA
    sink, corr = pl.pallas_call(
        kernel,
        out_shape=(
            jax.ShapeDtypeStruct(elementals.shape, BF16),
            jax.ShapeDtypeStruct((1, ops, ops, 2), F32),
        ),
        in_specs=[
            pl.BlockSpec(memory_space=pltpu.SMEM),
            pl.BlockSpec(memory_space=pltpu.SMEM),
            pl.BlockSpec(memory_space=pl.ANY),
            pl.BlockSpec(memory_space=pl.ANY),
        ],
        out_specs=(pl.BlockSpec(memory_space=pl.ANY), pl.BlockSpec(memory_space=pltpu.VMEM)),
        scratch_shapes=[
            *[pltpu.VMEM((slots, 2, rows, quarter), BF16)] * OPS,
            pltpu.VMEM((ops, 2, XS - 1, 2, rows, quarter), BF16),
            pltpu.VMEM((ops, 2, rows, order), BF16),
            pltpu.VMEM((ops, 2, rows, order), BF16),
            pltpu.VMEM((2, order, order), BF16),
            pltpu.VMEM((4 * rows, order), BF16),
            pltpu.VMEM((4 * rows, order), BF16),
            pltpu.VMEM((2, MODES, rows, 4 * rows), BF16),
            pltpu.VMEM((2, MODES, rows, 4 * rows), BF16),
            pltpu.VMEM((ops, 2, rows, order), BF16),
            pltpu.VMEM((XS, 8, 128), jnp.int32),
            pltpu.SMEM((XS, 8, 128), jnp.int32),
            pltpu.VMEM((MODES, ops * ops * 2, 128), F32),
            dma((XS - 1,)), dma((XS - 1,)),
            dma((OPS, XS - 1)), dma((OPS, XS - 1)),
            dma((OPS,)), dma((OPS,)),
            dma((OPS, 2, XS - 1)), dma((OPS, 2, XS - 1)),
            dma((24,)), dma((24,)),
            dma((2, MODES)), dma((2, MODES)),
            dma((MODES,)), dma((MODES,)),
            dma((2 + OPS + 2,)), dma((2,)),
        ],
        compiler_params=pltpu.CompilerParams(
            collective_id=0, has_side_effects=True, vmem_limit_bytes=56 << 20
        ),
        name="meson",
    )(time_pairs, slot_of, elementals, propagators)
    return corr, sink


def solution(mesh):
    in_specs = (
        P("pair", None),
        P(),
        P("pair", None, None, "mode", None),
        P("pair", None, "mode", None),
    )
    out_specs = (P("pair", None, None, None), P("pair", None, None, "mode", None))
    return jax.shard_map(body, mesh=mesh, in_specs=in_specs, out_specs=out_specs, check_vma=False)
```

```python
import functools

import jax
import jax.numpy as jnp
from jax import lax
from jax.experimental import pallas as pl
from jax.experimental.pallas import tpu as pltpu
from jax.sharding import PartitionSpec as P

MESH = pl.DeviceIdType.MESH
F32 = jnp.float32
BF16 = jnp.bfloat16
XS = 4
MODES = 16
OPS = 4
SLOTS = 8


def kernel(times, slots, elem_ref, prop_ref, sink_ref, corr_ref,
           r0, r1, r2, r3, staged, w_sink, w_source, tau, stack, stack2, turned, arrived, sink,
           want_all, want_smem, lines, parts,
           want_send, want_recv, p1_send, p1_recv, y_send, y_recv, p2_send, p2_recv,
           tau_send, tau_recv, t_send, t_recv, ps_send, ps_recv, local, out_sem):
    elem, prop, sink_hbm = elem_ref.at[0], prop_ref.at[0], sink_ref.at[0]
    rows = elem.shape[2]
    order = elem.shape[3]
    quarter = order // XS
    gathered = (r0, r1, r2, r3)

    pair = lax.axis_index("pair")
    mode = lax.axis_index("mode")
    yh, x = pair // XS, pair % XS
    yl, z, core = mode // 8, (mode // 2) % 4, mode % 2

    def at_x(step):
        return (yh * XS + (x + step) % XS, mode)

    y_partner = ((1 - yh) * XS + x, mode)

    def chunk(y_at, z_at, core_at):
        return y_at * 8 + z_at * 2 + core_at

    def at_mode(y_at, z_at, core_at):
        return (pair, chunk(y_at, z_at, core_at))

    def remote(src, dst, send, recv, device):
        return pltpu.make_async_remote_copy(
            src_ref=src, dst_ref=dst, send_sem=send, recv_sem=recv,
            device_id=device, device_id_type=MESH)

    line = lax.broadcasted_iota(jnp.int32, (8, 128), 0)
    want_all[x] = jnp.where(line == 0, slots[times[0, 0]], slots[times[0, 1]])

    barrier = pltpu.get_barrier_semaphore()
    for step in range(1, XS):
        pl.semaphore_signal(barrier, inc=1, device_id=at_x(step), device_id_type=MESH)
    pl.semaphore_signal(barrier, inc=1, device_id=y_partner, device_id_type=MESH)

    @pl.loop(1, MODES)
    def _(step):
        pl.semaphore_signal(barrier, inc=1, device_id=(pair, (mode + step) % MODES), device_id_type=MESH)

    pl.semaphore_wait(barrier, XS - 1 + 1 + MODES - 1)

    want_copies = [
        remote(want_all.at[x], want_all.at[x], want_send.at[s - 1], want_recv.at[s - 1], at_x(s))
        for s in range(1, XS)
    ]
    for copy in want_copies:
        copy.start()

    def columns(at):
        return pl.ds(pl.multiple_of(at * quarter, 128), quarter)

    def stage1(o):
        copies = []
        for s in (2, 1, 3):
            copies.append(remote(
                elem.at[o, :, :, columns((x + s) % XS)], gathered[o].at[pair],
                p1_send.at[o, s - 1], p1_recv.at[o, s - 1], at_x(s)))
        own = pltpu.make_async_copy(elem.at[o, :, :, columns(x)], gathered[o].at[pair], local.at[1 + o])
        return copies, own

    first = [stage1(o) for o in range(OPS)]

    half = rows // 2
    tau_copies = {}

    def tau_rows(index, start=0, size=rows):
        return tau.at[:, pl.ds(pl.multiple_of(index * rows + start, 16), size), :]

    def pass_on(name, src, dst, device):
        k = len(tau_copies)
        copy = remote(src, dst, tau_send.at[k], tau_recv.at[k], device)
        copy.start()
        tau_copies[name] = copy

    def pass_rows(name, index, device, start=0, size=rows):
        ref = tau_rows(index, start, size)
        pass_on(name, ref, ref, device)

    zp, zm, zf = (z + 1) % 4, (z + 3) % 4, (z + 2) % 4
    up, down, sibling = at_mode(yl, zp, core), at_mode(yl, zm, core), at_mode(yl, z, 1 - core)
    own_chunk = chunk(yl, z, core)

    for copy in first[0][0]:
        copy.start()
    first[0][1].start()
    pass_on("y", prop, tau_rows(own_chunk), at_mode(1 - yl, z, core))
    pass_on("z+", prop, tau_rows(own_chunk), up)
    pass_on("z-", prop, tau_rows(own_chunk), down)
    pass_on("c", prop, tau_rows(own_chunk), sibling)
    own_tau = pltpu.make_async_copy(prop, tau_rows(own_chunk), local.at[1 + OPS])
    own_tau.start()
    for o in range(1, OPS):
        for copy in first[o][0]:
            copy.start()
        first[o][1].start()

    plane = pl.ds(yh * XS, XS)
    across = [
        remote(gathered[o].at[plane], gathered[o].at[plane], y_send.at[o], y_recv.at[o], y_partner)
        for o in range(OPS)
    ]

    def stage2(o):
        copies, own = first[o]
        own.wait()
        for copy in copies:
            copy.wait_recv()
        across[o].start()

    second = {}

    def stage3(o):
        across[o].wait_recv()
        for k, held in ((1, w_source), (0, w_sink)):
            for s in (2, 1, 3):
                slot = want_smem[(x + s) % XS, k, 0]
                staged[o, k, s - 1] = gathered[o][slot]
                copy = remote(
                    staged.at[o, k, s - 1], held.at[o, :, :, columns(x)],
                    p2_send.at[o, k, s - 1], p2_recv.at[o, k, s - 1], at_x(s))
                copy.start()
                second[o, k, s] = copy
            held[o, :, :, columns(x)] = gathered[o][want_smem[x, k, 0]]

    def wait_stage3(o, k):
        for s in range(1, XS):
            second[o, k, s].wait_recv()

    def relay(letter, y_at):
        tau_copies[letter + "z+"].wait_recv()
        below = chunk(y_at, zm, core)
        pass_rows(letter + "h+", below, up, 0, half)
        pass_rows(letter + "cz+", below, sibling)
        tau_copies[letter + "z-"].wait_recv()
        above = chunk(y_at, zp, core)
        pass_rows(letter + "h-", above, down, half, half)
        pass_rows(letter + "cz-", above, sibling)

    def relay_far(letter, y_at):
        far = chunk(y_at, zf, core)
        tau_copies[letter + "h+"].wait_recv()
        pass_rows(letter + "ch+", far, sibling, 0, half)
        tau_copies[letter + "h-"].wait_recv()
        pass_rows(letter + "ch-", far, sibling, half, half)

    stage2(0)
    for copy in want_copies:
        copy.wait_recv()
    to_smem = pltpu.make_async_copy(want_all, want_smem, local.at[0])
    to_smem.start()
    stage2(1)
    tau_copies["y"].wait_recv()
    other = chunk(1 - yl, z, core)
    pass_rows("Vz+", other, up)
    pass_rows("Vz-", other, down)
    pass_rows("Vc", other, sibling)
    relay("", yl)
    stage2(2)
    to_smem.wait()
    stage3(0)
    relay_far("", yl)
    stage2(3)
    relay("V", 1 - yl)
    stage3(1)
    relay_far("V", 1 - yl)
    stage3(2)
    own_tau.wait()
    for name in ("c", "Vc", "cz+", "cz-", "Vcz+", "Vcz-", "ch+", "ch-", "Vch+", "Vch-"):
        tau_copies[name].wait_recv()

    span = 4 * rows
    dims = (((1,), (1,)), ((), ()))

    def source(h):
        for j in range(2):
            o = 2 * h + j
            wait_stage3(o, 1)
            real, imag = w_source[o, 0], w_source[o, 1]
            stack[pl.ds(2 * j * rows, rows), :] = real
            stack[pl.ds((2 * j + 1) * rows, rows), :] = -imag
            stack2[pl.ds(2 * j * rows, rows), :] = imag
            stack2[pl.ds((2 * j + 1) * rows, rows), :] = real

        @pl.loop(0, order // span)
        def _(step):
            i = (step + mode // 4 + 1) % 4
            at = pl.ds(pl.multiple_of(i * span, 16), span)
            total = lax.dot_general(tau[0, at, :], stack[...], dims, preferred_element_type=F32)
            total += lax.dot_general(tau[1, at, :], stack2[...], dims, preferred_element_type=F32)
            turned[h, pl.ds(i * 4, 4)] = total.astype(BF16).reshape(4, rows, span)

            @pl.loop(i * 4, i * 4 + 4)
            def _(to):
                @pl.when(to != mode)
                def _():
                    slab(h, to, mode).start()

        own_slab(h).start()

    def slab(h, to, sender):
        return remote(turned.at[h, to], arrived.at[h, sender], t_send.at[h, to], t_recv.at[h, sender], (pair, to))

    def own_slab(h):
        return pltpu.make_async_copy(turned.at[h, mode], arrived.at[h, mode], local.at[2 + OPS + h])

    wide = 256

    def sink_product(h):
        for j in range(2):
            o = 2 * h + j
            wait_stage3(o, 0)
            stack[pl.ds(2 * j * rows, rows), :] = -w_sink[o, 1]
            stack[pl.ds((2 * j + 1) * rows, rows), :] = w_sink[o, 0]

        @pl.loop(0, order // wide)
        def _(i):
            at = pl.ds(pl.multiple_of(i * wide, 128), wide)
            left = w_sink[2 * h:2 * h + 2].reshape(span, order)
            total = jnp.dot(left, tau[0, :, at], preferred_element_type=F32)
            total += jnp.dot(stack[...], tau[1, :, at], preferred_element_type=F32)
            sink[2 * h:2 * h + 2, :, :, at] = total.astype(BF16).reshape(2, 2, rows, wide)

        pltpu.make_async_copy(sink.at[pl.ds(2 * h, 2)], sink_hbm.at[pl.ds(2 * h, 2)], out_sem.at[h]).start()

    tall = 16

    def contract(h):
        group = lax.broadcasted_iota(jnp.int32, (tall, span), 1) // rows
        picks = [group == b for b in range(3)]

        def body(g, it, sums):
            sums = list(sums)
            row = pl.ds(pl.multiple_of(it * tall, tall), tall)
            blocks = [arrived[h, 4 * g + b, row, :].astype(F32) for b in range(4)]
            source_parts = []
            for a in range(4):
                moved = [
                    blocks[b] if a == b else pltpu.roll(blocks[b], (rows * (b - a)) % span, 1)
                    for b in range(4)
                ]
                source_parts.append(jnp.where(
                    picks[0], moved[0], jnp.where(picks[1], moved[1], jnp.where(picks[2], moved[2], moved[3]))))
            at = pl.ds(pl.multiple_of(g * span, 128), span)
            for o in range(OPS):
                s_re = sink[o, 0, row, at].astype(F32)
                s_im = sink[o, 1, row, at].astype(F32)
                for j in range(2):
                    t_re, t_im = source_parts[2 * j], source_parts[2 * j + 1]
                    for part, value in enumerate((s_re * t_re + s_im * t_im, s_im * t_re - s_re * t_im)):
                        value = value[:8] + value[8:]
                        value = value[:, :128] + value[:, 128:256] + value[:, 256:]
                        sums[(o * 2 + j) * 2 + part] += value
            return tuple(sums)

        def from_group(step, sums):
            g = (mode // 4 + step) % 4

            @pl.loop(4 * g, 4 * g + 4)
            def _(sender):
                @pl.when(sender != mode)
                def _():
                    slab(h, sender, sender).wait_recv()

            return lax.fori_loop(0, rows // tall, functools.partial(body, g), sums)

        own_slab(h).wait()
        zero = jnp.zeros((8, 128), F32)
        sums = lax.fori_loop(0, MODES // 4, from_group, (zero,) * (OPS * 4))
        for o in range(OPS):
            for j in range(2):
                for part in range(2):
                    index = (2 * h + j) * 2 * OPS + 2 * o + part
                    lines[index:index + 1, :] = jnp.sum(
                        sums[(o * 2 + j) * 2 + part], axis=0, keepdims=True)

    source(0)
    stage3(3)
    sink_product(0)
    source(1)
    sink_product(1)
    contract(0)
    contract(1)

    column = jnp.sum(lines[...], axis=1, keepdims=True)
    lane = lax.broadcasted_iota(jnp.int32, (2 * OPS, 128), 1)
    tile = jnp.zeros((2 * OPS, 128), F32)
    for q in range(OPS):
        tile = jnp.where(lane == q, column[2 * OPS * q:2 * OPS * (q + 1)], tile)
    parts[mode] = tile

    @pl.loop(1, MODES)
    def _(step):
        remote(parts.at[mode], parts.at[mode], ps_send.at[step], ps_recv.at[step],
               (pair, (mode + step) % MODES)).start()

    @pl.loop(1, MODES)
    def _(step):
        remote(parts.at[mode], parts.at[mode], ps_send.at[step], ps_recv.at[step],
               (pair, (mode + step) % MODES)).wait()

    total = parts[0]
    for n in range(1, MODES):
        total = total + parts[n]
    total = total * (1.0 / order)
    for o in range(OPS):
        corr_ref[0, o] = total[2 * o:2 * o + 2, :OPS]

    for copy in want_copies:
        copy.wait_send()
    for copies, _ in first:
        for copy in copies:
            copy.wait_send()
    for copy in across:
        copy.wait_send()
    for copy in second.values():
        copy.wait_send()
    for copy in tau_copies.values():
        copy.wait_send()
    for h in range(2):
        @pl.loop(0, MODES)
        def _(to):
            @pl.when(to != mode)
            def _():
                slab(h, to, mode).wait_send()

    for h in range(2):
        pltpu.make_async_copy(sink.at[pl.ds(2 * h, 2)], sink_hbm.at[pl.ds(2 * h, 2)], out_sem.at[h]).wait()


def body(time_pairs, slot_of, elementals, propagators):
    _, ops, parts, rows, order = elementals.shape
    slots = slot_of.shape[0]
    quarter = order // XS
    dma = pltpu.SemaphoreType.DMA
    sink, corr = pl.pallas_call(
        kernel,
        out_shape=(
            jax.ShapeDtypeStruct(elementals.shape, BF16),
            jax.ShapeDtypeStruct((1, ops, 2, ops), F32),
        ),
        in_specs=[
            pl.BlockSpec(memory_space=pltpu.SMEM),
            pl.BlockSpec(memory_space=pltpu.SMEM),
            pl.BlockSpec(memory_space=pl.ANY),
            pl.BlockSpec(memory_space=pl.ANY),
        ],
        out_specs=(pl.BlockSpec(memory_space=pl.ANY), pl.BlockSpec(memory_space=pltpu.VMEM)),
        scratch_shapes=[
            *[pltpu.VMEM((slots, 2, rows, quarter), BF16)] * OPS,
            pltpu.VMEM((ops, 2, XS - 1, 2, rows, quarter), BF16),
            pltpu.VMEM((ops, 2, rows, order), BF16),
            pltpu.VMEM((ops, 2, rows, order), BF16),
            pltpu.VMEM((2, order, order), BF16),
            pltpu.VMEM((4 * rows, order), BF16),
            pltpu.VMEM((4 * rows, order), BF16),
            pltpu.VMEM((2, MODES, rows, 4 * rows), BF16),
            pltpu.VMEM((2, MODES, rows, 4 * rows), BF16),
            pltpu.VMEM((ops, 2, rows, order), BF16),
            pltpu.VMEM((XS, 8, 128), jnp.int32),
            pltpu.SMEM((XS, 8, 128), jnp.int32),
            pltpu.VMEM((ops * ops * 2, 128), F32),
            pltpu.VMEM((MODES, 2 * ops, 128), F32),
            dma((XS - 1,)), dma((XS - 1,)),
            dma((OPS, XS - 1)), dma((OPS, XS - 1)),
            dma((OPS,)), dma((OPS,)),
            dma((OPS, 2, XS - 1)), dma((OPS, 2, XS - 1)),
            dma((24,)), dma((24,)),
            dma((2, MODES)), dma((2, MODES)),
            dma((MODES,)), dma((MODES,)),
            dma((2 + OPS + 2,)), dma((2,)),
        ],
        compiler_params=pltpu.CompilerParams(
            collective_id=0, has_side_effects=True, vmem_limit_bytes=56 << 20
        ),
        name="meson",
    )(time_pairs, slot_of, elementals, propagators)
    return jnp.swapaxes(corr, 2, 3), sink


def solution(mesh):
    in_specs = (
        P("pair", None),
        P(),
        P("pair", None, None, "mode", None),
        P("pair", None, "mode", None),
    )
    out_specs = (P("pair", None, None, None), P("pair", None, None, "mode", None))
    return jax.shard_map(body, mesh=mesh, in_specs=in_specs, out_specs=out_specs, check_vma=False)
```

```python
import jax
import jax.numpy as jnp
from jax import lax
from jax.experimental import pallas as pl
from jax.experimental.pallas import tpu as pltpu
from jax.sharding import PartitionSpec as P

MESH = pl.DeviceIdType.MESH
F32 = jnp.float32
BF16 = jnp.bfloat16
XS = 4
MODES = 16
OPS = 4
SLOTS = 8


def kernel(times, slots, elem_ref, prop_ref, sink_ref, corr_ref,
           r0, r1, r2, r3, staged, w_sink, w_source, tau, stack, stack2, left, turned, arrived, aligned,
           want_all, want_smem, lines, parts,
           want_send, want_recv, p1_send, p1_recv, y_send, y_recv, p2_send, p2_recv,
           tau_send, tau_recv, t_send, t_recv, ps_send, ps_recv, local):
    elem, prop, sink = elem_ref.at[0], prop_ref.at[0], sink_ref.at[0]
    rows = elem.shape[2]
    order = elem.shape[3]
    quarter = order // XS
    gathered = (r0, r1, r2, r3)

    pair = lax.axis_index("pair")
    mode = lax.axis_index("mode")
    yh, x = pair // XS, pair % XS
    yl, z, core = mode // 8, (mode // 2) % 4, mode % 2

    def at_x(step):
        return (yh * XS + (x + step) % XS, mode)

    y_partner = ((1 - yh) * XS + x, mode)

    def chunk(y_at, z_at, core_at):
        return y_at * 8 + z_at * 2 + core_at

    def at_mode(y_at, z_at, core_at):
        return (pair, chunk(y_at, z_at, core_at))

    def remote(src, dst, send, recv, device):
        return pltpu.make_async_remote_copy(
            src_ref=src, dst_ref=dst, send_sem=send, recv_sem=recv,
            device_id=device, device_id_type=MESH)

    line = lax.broadcasted_iota(jnp.int32, (8, 128), 0)
    want_all[x] = jnp.where(line == 0, slots[times[0, 0]], slots[times[0, 1]])

    barrier = pltpu.get_barrier_semaphore()
    for step in range(1, XS):
        pl.semaphore_signal(barrier, inc=1, device_id=at_x(step), device_id_type=MESH)
    pl.semaphore_signal(barrier, inc=1, device_id=y_partner, device_id_type=MESH)

    @pl.loop(1, MODES)
    def _(step):
        pl.semaphore_signal(barrier, inc=1, device_id=(pair, (mode + step) % MODES), device_id_type=MESH)

    pl.semaphore_wait(barrier, XS - 1 + 1 + MODES - 1)

    want_copies = [
        remote(want_all.at[x], want_all.at[x], want_send.at[s - 1], want_recv.at[s - 1], at_x(s))
        for s in range(1, XS)
    ]
    for copy in want_copies:
        copy.start()

    def columns(at):
        return pl.ds(pl.multiple_of(at * quarter, 128), quarter)

    def stage1(o):
        copies = []
        for s in (2, 1, 3):
            copies.append(remote(
                elem.at[o, :, :, columns((x + s) % XS)], gathered[o].at[pair],
                p1_send.at[o, s - 1], p1_recv.at[o, s - 1], at_x(s)))
        own = pltpu.make_async_copy(elem.at[o, :, :, columns(x)], gathered[o].at[pair], local.at[1 + o])
        return copies, own

    first = [stage1(o) for o in range(OPS)]

    half = rows // 2
    tau_copies = {}

    def tau_rows(index, start=0, size=rows):
        return tau.at[:, pl.ds(pl.multiple_of(index * rows + start, 16), size), :]

    def pass_on(name, src, dst, device):
        k = len(tau_copies)
        copy = remote(src, dst, tau_send.at[k], tau_recv.at[k], device)
        copy.start()
        tau_copies[name] = copy

    def pass_rows(name, index, device, start=0, size=rows):
        ref = tau_rows(index, start, size)
        pass_on(name, ref, ref, device)

    zp, zm, zf = (z + 1) % 4, (z + 3) % 4, (z + 2) % 4
    up, down, sibling = at_mode(yl, zp, core), at_mode(yl, zm, core), at_mode(yl, z, 1 - core)
    own_chunk = chunk(yl, z, core)

    for copy in first[0][0]:
        copy.start()
    first[0][1].start()
    pass_on("y", prop, tau_rows(own_chunk), at_mode(1 - yl, z, core))
    pass_on("z+", prop, tau_rows(own_chunk), up)
    pass_on("z-", prop, tau_rows(own_chunk), down)
    pass_on("c", prop, tau_rows(own_chunk), sibling)
    own_tau = pltpu.make_async_copy(prop, tau_rows(own_chunk), local.at[1 + OPS])
    own_tau.start()
    for o in range(1, OPS):
        for copy in first[o][0]:
            copy.start()
        first[o][1].start()

    plane = pl.ds(yh * XS, XS)
    across = [
        remote(gathered[o].at[plane], gathered[o].at[plane], y_send.at[o], y_recv.at[o], y_partner)
        for o in range(OPS)
    ]

    def stage2(o):
        copies, own = first[o]
        own.wait()
        for copy in copies:
            copy.wait_recv()
        across[o].start()

    second = {}

    def stage3(o):
        across[o].wait_recv()
        for k, held in ((1, w_source), (0, w_sink)):
            for s in (2, 1, 3):
                slot = want_smem[(x + s) % XS, k, 0]
                staged[o, k, s - 1] = gathered[o][slot]
                copy = remote(
                    staged.at[o, k, s - 1], held.at[o, :, :, columns(x)],
                    p2_send.at[o, k, s - 1], p2_recv.at[o, k, s - 1], at_x(s))
                copy.start()
                second[o, k, s] = copy
            held[o, :, :, columns(x)] = gathered[o][want_smem[x, k, 0]]

    def wait_stage3(o, k):
        for s in range(1, XS):
            second[o, k, s].wait_recv()

    def relay(letter, y_at):
        tau_copies[letter + "z+"].wait_recv()
        below = chunk(y_at, zm, core)
        pass_rows(letter + "h+", below, up, 0, half)
        pass_rows(letter + "cz+", below, sibling)
        tau_copies[letter + "z-"].wait_recv()
        above = chunk(y_at, zp, core)
        pass_rows(letter + "h-", above, down, half, half)
        pass_rows(letter + "cz-", above, sibling)

    def relay_far(letter, y_at):
        far = chunk(y_at, zf, core)
        tau_copies[letter + "h+"].wait_recv()
        pass_rows(letter + "ch+", far, sibling, 0, half)
        tau_copies[letter + "h-"].wait_recv()
        pass_rows(letter + "ch-", far, sibling, half, half)

    stage2(0)
    for copy in want_copies:
        copy.wait_recv()
    to_smem = pltpu.make_async_copy(want_all, want_smem, local.at[0])
    to_smem.start()
    stage2(1)
    tau_copies["y"].wait_recv()
    other = chunk(1 - yl, z, core)
    pass_rows("Vz+", other, up)
    pass_rows("Vz-", other, down)
    pass_rows("Vc", other, sibling)
    relay("", yl)
    stage2(2)
    to_smem.wait()
    stage3(0)
    relay_far("", yl)
    stage2(3)
    relay("V", 1 - yl)
    stage3(1)
    relay_far("V", 1 - yl)
    stage3(2)
    own_tau.wait()
    for name in ("c", "Vc", "cz+", "cz-", "Vcz+", "Vcz-", "ch+", "ch-", "Vch+", "Vch-"):
        tau_copies[name].wait_recv()

    span = 4 * rows
    dims = (((1,), (1,)), ((), ()))
    pad = stack.shape[0] - 2 * rows
    stack[pl.ds(2 * rows, pad), :] = jnp.zeros((pad, order), BF16)
    stack2[pl.ds(2 * rows, pad), :] = jnp.zeros((pad, order), BF16)

    def slab(o, to, sender):
        return remote(turned.at[o, to], arrived.at[o, sender], t_send.at[o, to], t_recv.at[o, sender], (pair, to))

    def own_slab(o):
        return pltpu.make_async_copy(turned.at[o, mode], arrived.at[o, mode], local.at[2 + OPS + o])

    def source(o):
        wait_stage3(o, 1)
        real, imag = w_source[o, 0], w_source[o, 1]
        stack[pl.ds(0, rows), :] = real
        stack[pl.ds(rows, rows), :] = -imag
        stack2[pl.ds(0, rows), :] = imag
        stack2[pl.ds(rows, rows), :] = real

        blocks = 2 if o == OPS - 1 else 1
        many = order // blocks
        owners = MODES // blocks

        @pl.loop(0, blocks)
        def _(i):
            at = pl.ds(pl.multiple_of(i * many, 16), many)
            total = lax.dot_general(tau[0, at, :], stack[...], dims, preferred_element_type=F32)
            total += lax.dot_general(tau[1, at, :], stack2[...], dims, preferred_element_type=F32)
            total = total.reshape(owners, 2, half, 2 * rows + pad)
            blank = jnp.zeros((owners * half, span - 2 * rows - pad), F32)
            upper = jnp.concatenate([total[:, 0].reshape(owners * half, 2 * rows + pad), blank], axis=1)
            lower = jnp.concatenate([blank, total[:, 1].reshape(owners * half, 2 * rows + pad)], axis=1)
            packed = upper + pltpu.roll(lower, pad, 1)
            turned[o, pl.ds(i * owners, owners)] = packed.astype(BF16).reshape(owners, half, span)

            @pl.loop(0, owners)
            def _(step):
                to = i * owners + (mode + step) % owners

                @pl.when(to != mode)
                def _():
                    slab(o, to, mode).start()

        own_slab(o).start()

    wide = 768

    def sink_product(o):
        wait_stage3(o, 0)
        left[pl.ds(0, rows), pl.ds(0, order)] = w_sink[o, 0]
        left[pl.ds(0, rows), pl.ds(order, order)] = -w_sink[o, 1]
        left[pl.ds(rows, rows), pl.ds(0, order)] = w_sink[o, 1]
        left[pl.ds(rows, rows), pl.ds(order, order)] = w_sink[o, 0]

        @pl.loop(0, order // wide)
        def _(i):
            at = pl.ds(pl.multiple_of(i * wide, 128), wide)
            total = jnp.dot(left[...], tau[:, :, at].reshape(2 * order, wide), preferred_element_type=F32)
            sink[o, :, :, at] = total.astype(BF16).reshape(2, rows, wide)

    tall = 16

    def align(o):
        group = lax.broadcasted_iota(jnp.int32, (tall, span), 1) // rows
        picks = [group == b for b in range(3)]
        own_slab(o).wait()

        @pl.loop(0, MODES // 4)
        def _(step):
            g = (mode // 4 + step) % 4

            @pl.loop(4 * g, 4 * g + 4)
            def _(sender):
                @pl.when(sender != mode)
                def _():
                    slab(o, sender, sender).wait_recv()

            @pl.loop(0, half // tall)
            def _(it):
                row = pl.ds(pl.multiple_of(it * tall, tall), tall)
                blocks = [arrived[o, 4 * g + b, row, :].astype(F32) for b in range(4)]
                for a in range(4):
                    moved = [
                        blocks[b] if a == b else pltpu.roll(blocks[b], (rows * (b - a)) % span, 1)
                        for b in range(4)
                    ]
                    part = jnp.where(
                        picks[0], moved[0], jnp.where(picks[1], moved[1], jnp.where(picks[2], moved[2], moved[3])))
                    down_to = pl.ds(pl.multiple_of((a // 2) * half + it * tall, tall), tall)
                    aligned[o, a % 2, down_to, pl.ds(pl.multiple_of(g * span, 128), span)] = part.astype(BF16)

    part_wide = 256

    def contract(os, qs):
        def body(it, sums):
            sums = list(sums)
            row = pl.ds(pl.multiple_of((it // 6) * tall, tall), tall)
            at = pl.ds(pl.multiple_of((it % 6) * part_wide, 128), part_wide)
            right = [(aligned[q, 0, row, at].astype(F32), aligned[q, 1, row, at].astype(F32)) for q in qs]
            k = 0
            for o in os:
                s_re, s_im = sink[o, 0, row, at].astype(F32), sink[o, 1, row, at].astype(F32)
                for t_re, t_im in right:
                    for value in (s_re * t_re + s_im * t_im, s_im * t_re - s_re * t_im):
                        value = value[:8] + value[8:]
                        sums[k] += value[:, :128] + value[:, 128:]
                        k += 1
            return tuple(sums)

        zero = jnp.zeros((8, 128), F32)
        sums = lax.fori_loop(0, (rows // tall) * (order // part_wide), body, (zero,) * (2 * len(os) * len(qs)))
        k = 0
        for o in os:
            for q in qs:
                for part in range(2):
                    index = q * 2 * OPS + 2 * o + part
                    lines[index:index + 1, :] = jnp.sum(sums[k], axis=0, keepdims=True)
                    k += 1

    source(0)
    sink_product(0)
    source(1)
    stage3(3)
    sink_product(1)
    align(0)
    source(2)
    sink_product(2)
    source(3)
    align(1)
    contract((0, 1, 2), (0, 1))
    sink_product(3)
    align(2)
    contract((3,), (0, 1))
    contract((0, 1, 2, 3), (2,))
    align(3)
    contract((0, 1, 2, 3), (3,))

    column = jnp.sum(lines[...], axis=1, keepdims=True)
    lane = lax.broadcasted_iota(jnp.int32, (2 * OPS, 128), 1)
    tile = jnp.zeros((2 * OPS, 128), F32)
    for q in range(OPS):
        tile = jnp.where(lane == q, column[2 * OPS * q:2 * OPS * (q + 1)], tile)
    parts[mode] = tile

    @pl.loop(1, MODES)
    def _(step):
        remote(parts.at[mode], parts.at[mode], ps_send.at[step], ps_recv.at[step],
               (pair, (mode + step) % MODES)).start()

    @pl.loop(1, MODES)
    def _(step):
        remote(parts.at[mode], parts.at[mode], ps_send.at[step], ps_recv.at[step],
               (pair, (mode + step) % MODES)).wait()

    total = parts[0]
    for n in range(1, MODES):
        total = total + parts[n]
    total = total * (1.0 / order)
    for o in range(OPS):
        corr_ref[0, o] = total[2 * o:2 * o + 2, :OPS]

    for copy in want_copies:
        copy.wait_send()
    for copies, _ in first:
        for copy in copies:
            copy.wait_send()
    for copy in across:
        copy.wait_send()
    for copy in second.values():
        copy.wait_send()
    for copy in tau_copies.values():
        copy.wait_send()
    for o in range(OPS):
        @pl.loop(0, MODES)
        def _(to):
            @pl.when(to != mode)
            def _():
                slab(o, to, mode).wait_send()


def body(time_pairs, slot_of, elementals, propagators):
    _, ops, parts, rows, order = elementals.shape
    slots = slot_of.shape[0]
    quarter = order // XS
    dma = pltpu.SemaphoreType.DMA
    sink, corr = pl.pallas_call(
        kernel,
        out_shape=(
            pltpu.VMEM(elementals.shape, BF16),
            pltpu.VMEM((1, ops, 2, ops), F32),
        ),
        in_specs=[
            pl.BlockSpec(memory_space=pltpu.SMEM),
            pl.BlockSpec(memory_space=pltpu.SMEM),
            pl.BlockSpec(memory_space=pl.ANY),
            pl.BlockSpec(memory_space=pl.ANY),
        ],
        out_specs=(pl.BlockSpec(memory_space=pltpu.VMEM), pl.BlockSpec(memory_space=pltpu.VMEM)),
        scratch_shapes=[
            *[pltpu.VMEM((slots, 2, rows, quarter), BF16)] * OPS,
            pltpu.VMEM((ops, 2, XS - 1, 2, rows, quarter), BF16),
            pltpu.VMEM((ops, 2, rows, order), BF16),
            pltpu.VMEM((ops, 2, rows, order), BF16),
            pltpu.VMEM((2, order, order), BF16),
            pltpu.VMEM((256, order), BF16),
            pltpu.VMEM((256, order), BF16),
            pltpu.VMEM((2 * rows, 2 * order), BF16),
            pltpu.VMEM((ops, MODES, rows // 2, 4 * rows), BF16),
            pltpu.VMEM((ops, MODES, rows // 2, 4 * rows), BF16),
            pltpu.VMEM((ops, 2, rows, order), BF16),
            pltpu.VMEM((XS, 8, 128), jnp.int32),
            pltpu.SMEM((XS, 8, 128), jnp.int32),
            pltpu.VMEM((ops * ops * 2, 128), F32),
            pltpu.VMEM((MODES, 2 * ops, 128), F32),
            dma((XS - 1,)), dma((XS - 1,)),
            dma((OPS, XS - 1)), dma((OPS, XS - 1)),
            dma((OPS,)), dma((OPS,)),
            dma((OPS, 2, XS - 1)), dma((OPS, 2, XS - 1)),
            dma((24,)), dma((24,)),
            dma((OPS, MODES)), dma((OPS, MODES)),
            dma((MODES,)), dma((MODES,)),
            dma((2 + OPS + OPS,)),
        ],
        compiler_params=pltpu.CompilerParams(
            collective_id=0, has_side_effects=True, vmem_limit_bytes=56 << 20
        ),
        name="meson",
    )(time_pairs, slot_of, elementals, propagators)
    return jnp.swapaxes(corr, 2, 3), sink


def solution(mesh):
    in_specs = (
        P("pair", None),
        P(),
        P("pair", None, None, "mode", None),
        P("pair", None, "mode", None),
    )
    out_specs = (P("pair", None, None, None), P("pair", None, None, "mode", None))
    return jax.shard_map(body, mesh=mesh, in_specs=in_specs, out_specs=out_specs, check_vma=False)
```

```python
import jax
import jax.numpy as jnp
from jax import lax
from jax.experimental import pallas as pl
from jax.experimental.pallas import tpu as pltpu
from jax.sharding import PartitionSpec as P

MESH = pl.DeviceIdType.MESH
F32 = jnp.float32
BF16 = jnp.bfloat16
XS = 4
MODES = 16
OPS = 4
SLOTS = 8


def kernel(times_ref, slots_ref, elem_ref, prop_ref, sink_ref, corr_ref,
           r0, r1, r2, r3, staged, w_sink, w_source, tau, stack, stack2, left, turned, arrived, aligned,
           times, slots, want_all, want_smem, lines, parts,
           want_send, want_recv, p1_send, p1_recv, y_send, y_recv, p2_send, p2_recv,
           tau_send, tau_recv, t_send, t_recv, ps_send, ps_recv, local):
    elem, prop, sink = elem_ref.at[0], prop_ref.at[0], sink_ref.at[0]
    rows = elem.shape[2]
    order = elem.shape[3]
    quarter = order // XS
    gathered = (r0, r1, r2, r3)

    pair = lax.axis_index("pair")
    mode = lax.axis_index("mode")
    yh, x = pair // XS, pair % XS
    yl, z, core = mode // 8, (mode // 2) % 4, mode % 2

    def at_x(step):
        return (yh * XS + (x + step) % XS, mode)

    y_partner = ((1 - yh) * XS + x, mode)

    def chunk(y_at, z_at, core_at):
        return y_at * 8 + z_at * 2 + core_at

    def at_mode(y_at, z_at, core_at):
        return (pair, chunk(y_at, z_at, core_at))

    def remote(src, dst, send, recv, device):
        return pltpu.make_async_remote_copy(
            src_ref=src, dst_ref=dst, send_sem=send, recv_sem=recv,
            device_id=device, device_id_type=MESH)

    load_times = pltpu.make_async_copy(times_ref, times, local.at[0])
    load_slots = pltpu.make_async_copy(slots_ref, slots, local.at[2 + 2 * OPS])
    load_times.start()
    load_slots.start()

    barrier = pltpu.get_barrier_semaphore()
    for step in range(1, XS):
        pl.semaphore_signal(barrier, inc=1, device_id=at_x(step), device_id_type=MESH)
    pl.semaphore_signal(barrier, inc=1, device_id=y_partner, device_id_type=MESH)

    @pl.loop(1, MODES)
    def _(step):
        pl.semaphore_signal(barrier, inc=1, device_id=(pair, (mode + step) % MODES), device_id_type=MESH)

    pl.semaphore_wait(barrier, XS - 1 + 1 + MODES - 1)

    def columns(at):
        return pl.ds(pl.multiple_of(at * quarter, 128), quarter)

    def stage1(o):
        copies = []
        for s in (2, 1, 3):
            copies.append(remote(
                elem.at[o, :, :, columns((x + s) % XS)], gathered[o].at[pair],
                p1_send.at[o, s - 1], p1_recv.at[o, s - 1], at_x(s)))
        own = pltpu.make_async_copy(elem.at[o, :, :, columns(x)], gathered[o].at[pair], local.at[1 + o])
        return copies, own

    first = [stage1(o) for o in range(OPS)]

    half = rows // 2
    tau_copies = {}

    def tau_rows(index, start=0, size=rows):
        return tau.at[:, pl.ds(pl.multiple_of(index * rows + start, 16), size), :]

    def pass_on(name, src, dst, device):
        k = len(tau_copies)
        copy = remote(src, dst, tau_send.at[k], tau_recv.at[k], device)
        copy.start()
        tau_copies[name] = copy

    def pass_rows(name, index, device, start=0, size=rows):
        ref = tau_rows(index, start, size)
        pass_on(name, ref, ref, device)

    zp, zm, zf = (z + 1) % 4, (z + 3) % 4, (z + 2) % 4
    up, down, sibling = at_mode(yl, zp, core), at_mode(yl, zm, core), at_mode(yl, z, 1 - core)
    own_chunk = chunk(yl, z, core)

    pass_on("y", prop, tau_rows(own_chunk), at_mode(1 - yl, z, core))
    for copy in first[0][0]:
        copy.start()
    first[0][1].start()
    pass_on("z+", prop, tau_rows(own_chunk), up)
    pass_on("z-", prop, tau_rows(own_chunk), down)
    pass_on("c", prop, tau_rows(own_chunk), sibling)
    own_tau = pltpu.make_async_copy(prop, tau_rows(own_chunk), local.at[1 + OPS])
    own_tau.start()
    for copy in first[1][0]:
        copy.start()
    first[1][1].start()

    load_times.wait()
    load_slots.wait()
    line = lax.broadcasted_iota(jnp.int32, (8, 128), 0)
    want_all[x] = jnp.where(line == 0, slots[times[0, 0]], slots[times[0, 1]])
    want_copies = [
        remote(want_all.at[x], want_all.at[x], want_send.at[s - 1], want_recv.at[s - 1], at_x(s))
        for s in range(1, XS)
    ]
    for copy in want_copies:
        copy.start()
    for o in range(2, OPS):
        for copy in first[o][0]:
            copy.start()
        first[o][1].start()

    plane = pl.ds(yh * XS, XS)
    across = [
        remote(gathered[o].at[plane], gathered[o].at[plane], y_send.at[o], y_recv.at[o], y_partner)
        for o in range(OPS)
    ]

    def stage2(o):
        copies, own = first[o]
        own.wait()
        for copy in copies:
            copy.wait_recv()
        across[o].start()

    second = {}

    def stage3(o):
        across[o].wait_recv()
        for k, held in ((1, w_source), (0, w_sink)):
            for s in (2, 1, 3):
                slot = want_smem[(x + s) % XS, k, 0]
                staged[o, k, s - 1] = gathered[o][slot]
                copy = remote(
                    staged.at[o, k, s - 1], held.at[o, :, :, columns(x)],
                    p2_send.at[o, k, s - 1], p2_recv.at[o, k, s - 1], at_x(s))
                copy.start()
                second[o, k, s] = copy
            held[o, :, :, columns(x)] = gathered[o][want_smem[x, k, 0]]

    def wait_stage3(o, k):
        for s in range(1, XS):
            second[o, k, s].wait_recv()

    def relay(letter, y_at):
        tau_copies[letter + "z+"].wait_recv()
        below = chunk(y_at, zm, core)
        pass_rows(letter + "h+", below, up, 0, half)
        pass_rows(letter + "cz+", below, sibling)
        tau_copies[letter + "z-"].wait_recv()
        above = chunk(y_at, zp, core)
        pass_rows(letter + "h-", above, down, half, half)
        pass_rows(letter + "cz-", above, sibling)

    def relay_far(letter, y_at):
        far = chunk(y_at, zf, core)
        tau_copies[letter + "h+"].wait_recv()
        pass_rows(letter + "ch+", far, sibling, 0, half)
        tau_copies[letter + "h-"].wait_recv()
        pass_rows(letter + "ch-", far, sibling, half, half)

    stage2(0)
    for copy in want_copies:
        copy.wait_recv()
    to_smem = pltpu.make_async_copy(want_all, want_smem, local.at[0])
    to_smem.start()
    stage2(1)
    tau_copies["y"].wait_recv()
    other = chunk(1 - yl, z, core)
    pass_rows("Vz+", other, up)
    pass_rows("Vz-", other, down)
    pass_rows("Vc", other, sibling)
    relay("", yl)
    stage2(2)
    to_smem.wait()
    stage3(0)
    relay_far("", yl)
    stage2(3)
    relay("V", 1 - yl)
    stage3(1)
    relay_far("V", 1 - yl)
    stage3(2)
    own_tau.wait()
    for name in ("c", "Vc", "cz+", "cz-", "Vcz+", "Vcz-", "ch+", "ch-", "Vch+", "Vch-"):
        tau_copies[name].wait_recv()

    span = 4 * rows
    dims = (((1,), (1,)), ((), ()))
    pad = stack.shape[0] - 2 * rows
    stack[pl.ds(2 * rows, pad), :] = jnp.zeros((pad, order), BF16)
    stack2[pl.ds(2 * rows, pad), :] = jnp.zeros((pad, order), BF16)

    def slab(o, to, sender):
        return remote(turned.at[o, to], arrived.at[o, sender], t_send.at[o, to], t_recv.at[o, sender], (pair, to))

    def own_slab(o):
        return pltpu.make_async_copy(turned.at[o, mode], arrived.at[o, mode], local.at[2 + OPS + o])

    def source(o):
        wait_stage3(o, 1)
        real, imag = w_source[o, 0], w_source[o, 1]
        stack[pl.ds(0, rows), :] = real
        stack[pl.ds(rows, rows), :] = -imag
        stack2[pl.ds(0, rows), :] = imag
        stack2[pl.ds(rows, rows), :] = real

        blocks = 2 if o == OPS - 1 else 1
        many = order // blocks
        owners = MODES // blocks

        @pl.loop(0, blocks)
        def _(i):
            at = pl.ds(pl.multiple_of(i * many, 16), many)
            total = lax.dot_general(tau[0, at, :], stack[...], dims, preferred_element_type=F32)
            total += lax.dot_general(tau[1, at, :], stack2[...], dims, preferred_element_type=F32)
            total = total.reshape(owners, 2, half, 2 * rows + pad)
            blank = jnp.zeros((owners * half, span - 2 * rows - pad), F32)
            upper = jnp.concatenate([total[:, 0].reshape(owners * half, 2 * rows + pad), blank], axis=1)
            lower = jnp.concatenate([blank, total[:, 1].reshape(owners * half, 2 * rows + pad)], axis=1)
            packed = upper + pltpu.roll(lower, pad, 1)
            turned[o, pl.ds(i * owners, owners)] = packed.astype(BF16).reshape(owners, half, span)

            @pl.loop(0, owners)
            def _(step):
                to = i * owners + (mode + step) % owners

                @pl.when(to != mode)
                def _():
                    slab(o, to, mode).start()

        own_slab(o).start()

    wide = 768

    def sink_product(o):
        wait_stage3(o, 0)
        left[pl.ds(0, rows), pl.ds(0, order)] = w_sink[o, 0]
        left[pl.ds(0, rows), pl.ds(order, order)] = -w_sink[o, 1]
        left[pl.ds(rows, rows), pl.ds(0, order)] = w_sink[o, 1]
        left[pl.ds(rows, rows), pl.ds(order, order)] = w_sink[o, 0]

        @pl.loop(0, order // wide)
        def _(i):
            at = pl.ds(pl.multiple_of(i * wide, 128), wide)
            total = jnp.dot(left[...], tau[:, :, at].reshape(2 * order, wide), preferred_element_type=F32)
            sink[o, :, :, at] = total.astype(BF16).reshape(2, rows, wide)

    tall = 16

    def align(o, then=None, start=()):
        group = lax.broadcasted_iota(jnp.int32, (tall, span), 1) // rows
        picks = [group == b for b in range(3)]
        own_slab(o).wait()

        def from_group(step, sums):
            g = (mode // 4 + step) % 4

            @pl.loop(4 * g, 4 * g + 4)
            def _(sender):
                @pl.when(sender != mode)
                def _():
                    slab(o, sender, sender).wait_recv()

            @pl.loop(0, half // tall)
            def _(it):
                row = pl.ds(pl.multiple_of(it * tall, tall), tall)
                blocks = [arrived[o, 4 * g + b, row, :].astype(F32) for b in range(4)]
                for a in range(4):
                    moved = [
                        blocks[b] if a == b else pltpu.roll(blocks[b], (rows * (b - a)) % span, 1)
                        for b in range(4)
                    ]
                    part = jnp.where(
                        picks[0], moved[0], jnp.where(picks[1], moved[1], jnp.where(picks[2], moved[2], moved[3])))
                    down_to = pl.ds(pl.multiple_of((a // 2) * half + it * tall, tall), tall)
                    aligned[o, a % 2, down_to, pl.ds(pl.multiple_of(g * span, 128), span)] = part.astype(BF16)

            return sums if then is None else then(g, sums)

        return lax.fori_loop(0, MODES // 4, from_group, start)

    def terms(os, qs, at, sums):
        wide = at.size

        def body(it, sums):
            sums = list(sums)
            row = pl.ds(pl.multiple_of(it * tall, tall), tall)
            right = [(aligned[q, 0, row, at].astype(F32), aligned[q, 1, row, at].astype(F32)) for q in qs]
            k = 0
            for o in os:
                s_re, s_im = sink[o, 0, row, at].astype(F32), sink[o, 1, row, at].astype(F32)
                for t_re, t_im in right:
                    for value in (s_re * t_re + s_im * t_im, s_im * t_re - s_re * t_im):
                        value = value[:8] + value[8:]
                        for lanes in range(0, wide, 128):
                            sums[k] += value[:, lanes:lanes + 128]
                        k += 1
            return tuple(sums)

        return lax.fori_loop(0, rows // tall, body, sums)

    def blank_sums(os, qs):
        return (jnp.zeros((8, 128), F32),) * (2 * len(os) * len(qs))

    def keep(os, qs, sums):
        k = 0
        for o in os:
            for q in qs:
                for part in range(2):
                    index = q * 2 * OPS + 2 * o + part
                    lines[index:index + 1, :] = jnp.sum(sums[k], axis=0, keepdims=True)
                    k += 1

    def contract(os, qs):
        def body(it, sums):
            return terms(os, qs, pl.ds(pl.multiple_of(it * 256, 128), 256), sums)

        keep(os, qs, lax.fori_loop(0, order // 256, body, blank_sums(os, qs)))

    def align_and_contract(o, os):
        def then(g, sums):
            return terms(os, (o,), pl.ds(pl.multiple_of(g * span, 128), span), sums)

        keep(os, (o,), align(o, then, blank_sums(os, (o,))))

    source(0)
    sink_product(0)
    source(1)
    stage3(3)
    sink_product(1)
    align(0)
    source(2)
    sink_product(2)
    source(3)
    align(1)
    contract((0, 1, 2), (0, 1))
    sink_product(3)
    align(2)
    contract((3,), (0, 1))
    contract((0, 1, 2, 3), (2,))
    align_and_contract(3, (0, 1, 2, 3))

    column = jnp.sum(lines[...], axis=1, keepdims=True)
    lane = lax.broadcasted_iota(jnp.int32, (2 * OPS, 128), 1)
    tile = jnp.zeros((2 * OPS, 128), F32)
    for q in range(OPS):
        tile = jnp.where(lane == q, column[2 * OPS * q:2 * OPS * (q + 1)], tile)
    parts[mode] = tile

    @pl.loop(1, MODES)
    def _(step):
        remote(parts.at[mode], parts.at[mode], ps_send.at[step], ps_recv.at[step],
               (pair, (mode + step) % MODES)).start()

    @pl.loop(1, MODES)
    def _(step):
        remote(parts.at[mode], parts.at[mode], ps_send.at[step], ps_recv.at[step],
               (pair, (mode + step) % MODES)).wait()

    total = parts[0]
    for n in range(1, MODES):
        total = total + parts[n]
    total = total * (1.0 / order)
    for o in range(OPS):
        corr_ref[0, o] = total[2 * o:2 * o + 2, :OPS]

    for copy in want_copies:
        copy.wait_send()
    for copies, _ in first:
        for copy in copies:
            copy.wait_send()
    for copy in across:
        copy.wait_send()
    for copy in second.values():
        copy.wait_send()
    for copy in tau_copies.values():
        copy.wait_send()
    for o in range(OPS):
        @pl.loop(0, MODES)
        def _(to):
            @pl.when(to != mode)
            def _():
                slab(o, to, mode).wait_send()


def body(time_pairs, slot_of, elementals, propagators):
    _, ops, parts, rows, order = elementals.shape
    slots = slot_of.shape[0]
    quarter = order // XS
    dma = pltpu.SemaphoreType.DMA
    sink, corr = pl.pallas_call(
        kernel,
        out_shape=(
            pltpu.VMEM(elementals.shape, BF16),
            pltpu.VMEM((1, ops, 2, ops), F32),
        ),
        in_specs=[
            pl.BlockSpec(memory_space=pl.ANY),
            pl.BlockSpec(memory_space=pl.ANY),
            pl.BlockSpec(memory_space=pl.ANY),
            pl.BlockSpec(memory_space=pl.ANY),
        ],
        out_specs=(pl.BlockSpec(memory_space=pltpu.VMEM), pl.BlockSpec(memory_space=pltpu.VMEM)),
        scratch_shapes=[
            *[pltpu.VMEM((slots, 2, rows, quarter), BF16)] * OPS,
            pltpu.VMEM((ops, 2, XS - 1, 2, rows, quarter), BF16),
            pltpu.VMEM((ops, 2, rows, order), BF16),
            pltpu.VMEM((ops, 2, rows, order), BF16),
            pltpu.VMEM((2, order, order), BF16),
            pltpu.VMEM((256, order), BF16),
            pltpu.VMEM((256, order), BF16),
            pltpu.VMEM((2 * rows, 2 * order), BF16),
            pltpu.VMEM((ops, MODES, rows // 2, 4 * rows), BF16),
            pltpu.VMEM((ops, MODES, rows // 2, 4 * rows), BF16),
            pltpu.VMEM((ops, 2, rows, order), BF16),
            pltpu.SMEM(time_pairs.shape, jnp.int32),
            pltpu.SMEM(slot_of.shape, jnp.int32),
            pltpu.VMEM((XS, 8, 128), jnp.int32),
            pltpu.SMEM((XS, 8, 128), jnp.int32),
            pltpu.VMEM((ops * ops * 2, 128), F32),
            pltpu.VMEM((MODES, 2 * ops, 128), F32),
            dma((XS - 1,)), dma((XS - 1,)),
            dma((OPS, XS - 1)), dma((OPS, XS - 1)),
            dma((OPS,)), dma((OPS,)),
            dma((OPS, 2, XS - 1)), dma((OPS, 2, XS - 1)),
            dma((24,)), dma((24,)),
            dma((OPS, MODES)), dma((OPS, MODES)),
            dma((MODES,)), dma((MODES,)),
            dma((3 + OPS + OPS,)),
        ],
        compiler_params=pltpu.CompilerParams(
            collective_id=0, has_side_effects=True, vmem_limit_bytes=56 << 20
        ),
        name="meson",
    )(time_pairs, slot_of, elementals, propagators)
    return jnp.swapaxes(corr, 2, 3), sink


def solution(mesh):
    in_specs = (
        P("pair", None),
        P(),
        P("pair", None, None, "mode", None),
        P("pair", None, "mode", None),
    )
    out_specs = (P("pair", None, None, None), P("pair", None, None, "mode", None))
    return jax.shard_map(body, mesh=mesh, in_specs=in_specs, out_specs=out_specs, check_vma=False)
```

```python
import jax
import jax.numpy as jnp
from jax import lax
from jax.experimental import pallas as pl
from jax.experimental.pallas import tpu as pltpu
from jax.sharding import PartitionSpec as P

MESH = pl.DeviceIdType.MESH
F32 = jnp.float32
BF16 = jnp.bfloat16
XS = 4
MODES = 16
OPS = 4
SLOTS = 8


def kernel(times_ref, slots_ref, elem_ref, prop_ref, sink_ref, corr_ref,
           r0, r1, r2, r3, staged, w_sink, w_source, tau, stack, stack2, left, turned, arrived, aligned,
           times, slots, want_all, want_smem, lines, parts,
           want_send, want_recv, p1_send, p1_recv, y_send, y_recv, p2_send, p2_recv,
           tau_send, tau_recv, t_send, t_recv, ps_send, ps_recv, local):
    elem, prop, sink = elem_ref.at[0], prop_ref.at[0], sink_ref.at[0]
    rows = elem.shape[2]
    order = elem.shape[3]
    quarter = order // XS
    gathered = (r0, r1, r2, r3)

    pair = lax.axis_index("pair")
    mode = lax.axis_index("mode")
    yh, x = pair // XS, pair % XS
    yl, z, core = mode // 8, (mode // 2) % 4, mode % 2

    def at_x(step):
        return (yh * XS + (x + step) % XS, mode)

    y_partner = ((1 - yh) * XS + x, mode)

    def chunk(y_at, z_at, core_at):
        return y_at * 8 + z_at * 2 + core_at

    def at_mode(y_at, z_at, core_at):
        return (pair, chunk(y_at, z_at, core_at))

    def remote(src, dst, send, recv, device):
        return pltpu.make_async_remote_copy(
            src_ref=src, dst_ref=dst, send_sem=send, recv_sem=recv,
            device_id=device, device_id_type=MESH)

    load_times = pltpu.make_async_copy(times_ref, times, local.at[0])
    load_slots = pltpu.make_async_copy(slots_ref, slots, local.at[2 + 2 * OPS])
    load_times.start()
    load_slots.start()

    barrier = pltpu.get_barrier_semaphore()
    for step in range(1, XS):
        pl.semaphore_signal(barrier, inc=1, device_id=at_x(step), device_id_type=MESH)
    pl.semaphore_signal(barrier, inc=1, device_id=y_partner, device_id_type=MESH)

    @pl.loop(1, MODES)
    def _(step):
        pl.semaphore_signal(barrier, inc=1, device_id=(pair, (mode + step) % MODES), device_id_type=MESH)

    pl.semaphore_wait(barrier, XS - 1 + 1 + MODES - 1)

    def columns(at):
        return pl.ds(pl.multiple_of(at * quarter, 128), quarter)

    def stage1(o):
        copies = []
        for s in (2, 1, 3):
            copies.append(remote(
                elem.at[o, :, :, columns((x + s) % XS)], gathered[o].at[pair],
                p1_send.at[o, s - 1], p1_recv.at[o, s - 1], at_x(s)))
        own = pltpu.make_async_copy(elem.at[o, :, :, columns(x)], gathered[o].at[pair], local.at[1 + o])
        return copies, own

    first = [stage1(o) for o in range(OPS)]

    half = rows // 2
    tau_copies = {}

    def tau_rows(index, start=0, size=rows):
        return tau.at[:, pl.ds(pl.multiple_of(index * rows + start, 16), size), :]

    def pass_on(name, src, dst, device):
        k = len(tau_copies)
        copy = remote(src, dst, tau_send.at[k], tau_recv.at[k], device)
        copy.start()
        tau_copies[name] = copy

    def pass_rows(name, index, device, start=0, size=rows):
        ref = tau_rows(index, start, size)
        pass_on(name, ref, ref, device)

    zp, zm, zf = (z + 1) % 4, (z + 3) % 4, (z + 2) % 4
    up, down, sibling = at_mode(yl, zp, core), at_mode(yl, zm, core), at_mode(yl, z, 1 - core)
    own_chunk = chunk(yl, z, core)

    pass_on("y", prop, tau_rows(own_chunk), at_mode(1 - yl, z, core))
    for copy in first[0][0]:
        copy.start()
    first[0][1].start()
    pass_on("z+", prop, tau_rows(own_chunk), up)
    pass_on("z-", prop, tau_rows(own_chunk), down)
    pass_on("c", prop, tau_rows(own_chunk), sibling)
    own_tau = pltpu.make_async_copy(prop, tau_rows(own_chunk), local.at[1 + OPS])
    own_tau.start()
    for copy in first[1][0]:
        copy.start()
    first[1][1].start()

    load_times.wait()
    load_slots.wait()
    line = lax.broadcasted_iota(jnp.int32, (8, 128), 0)
    want_all[x] = jnp.where(line == 0, slots[times[0, 0]], slots[times[0, 1]])
    want_copies = [
        remote(want_all.at[x], want_all.at[x], want_send.at[s - 1], want_recv.at[s - 1], at_x(s))
        for s in range(1, XS)
    ]
    for copy in want_copies:
        copy.start()
    for o in range(2, OPS):
        for copy in first[o][0]:
            copy.start()
        first[o][1].start()

    plane = pl.ds(yh * XS, XS)
    across = [
        remote(gathered[o].at[plane], gathered[o].at[plane], y_send.at[o], y_recv.at[o], y_partner)
        for o in range(OPS)
    ]

    def stage2(o):
        copies, own = first[o]
        own.wait()
        for copy in copies:
            copy.wait_recv()
        across[o].start()

    second = {}

    def stage3(o):
        across[o].wait_recv()
        for k, held in ((1, w_source), (0, w_sink)):
            for s in (2, 1, 3):
                slot = want_smem[(x + s) % XS, k, 0]
                staged[o, k, s - 1] = gathered[o][slot]
                copy = remote(
                    staged.at[o, k, s - 1], held.at[o, :, :, columns(x)],
                    p2_send.at[o, k, s - 1], p2_recv.at[o, k, s - 1], at_x(s))
                copy.start()
                second[o, k, s] = copy
            held[o, :, :, columns(x)] = gathered[o][want_smem[x, k, 0]]

    def wait_stage3(o, k):
        for s in range(1, XS):
            second[o, k, s].wait_recv()

    def relay(letter, y_at):
        tau_copies[letter + "z+"].wait_recv()
        below = chunk(y_at, zm, core)
        pass_rows(letter + "h+", below, up, 0, half)
        pass_rows(letter + "cz+", below, sibling)
        tau_copies[letter + "z-"].wait_recv()
        above = chunk(y_at, zp, core)
        pass_rows(letter + "h-", above, down, half, half)
        pass_rows(letter + "cz-", above, sibling)

    def relay_far(letter, y_at):
        far = chunk(y_at, zf, core)
        tau_copies[letter + "h+"].wait_recv()
        pass_rows(letter + "ch+", far, sibling, 0, half)
        tau_copies[letter + "h-"].wait_recv()
        pass_rows(letter + "ch-", far, sibling, half, half)

    stage2(0)
    for copy in want_copies:
        copy.wait_recv()
    to_smem = pltpu.make_async_copy(want_all, want_smem, local.at[0])
    to_smem.start()
    stage2(1)
    tau_copies["y"].wait_recv()
    other = chunk(1 - yl, z, core)
    pass_rows("Vz+", other, up)
    pass_rows("Vz-", other, down)
    pass_rows("Vc", other, sibling)
    relay("", yl)
    stage2(2)
    to_smem.wait()
    stage3(0)
    relay_far("", yl)
    stage2(3)
    relay("V", 1 - yl)
    stage3(1)
    relay_far("V", 1 - yl)
    stage3(2)
    own_tau.wait()
    for name in ("c", "Vc", "cz+", "cz-", "Vcz+", "Vcz-", "ch+", "ch-", "Vch+", "Vch-"):
        tau_copies[name].wait_recv()

    span = 4 * rows
    dims = (((1,), (1,)), ((), ()))
    pad = stack.shape[0] - 2 * rows
    stack[pl.ds(2 * rows, pad), :] = jnp.zeros((pad, order), BF16)
    stack2[pl.ds(2 * rows, pad), :] = jnp.zeros((pad, order), BF16)

    def slab(o, to, sender):
        return remote(turned.at[o, to], arrived.at[o, sender], t_send.at[o, to], t_recv.at[o, sender], (pair, to))

    def own_slab(o):
        return pltpu.make_async_copy(turned.at[o, mode], arrived.at[o, mode], local.at[2 + OPS + o])

    def source(o):
        wait_stage3(o, 1)
        real, imag = w_source[o, 0], w_source[o, 1]
        stack[pl.ds(0, rows), :] = real
        stack[pl.ds(rows, rows), :] = -imag
        stack2[pl.ds(0, rows), :] = imag
        stack2[pl.ds(rows, rows), :] = real

        blocks = 2
        many = order // blocks
        owners = MODES // blocks

        @pl.loop(0, blocks)
        def _(count):
            i = (1 - yl + count) % 2
            at = pl.ds(pl.multiple_of(i * many, 16), many)
            total = lax.dot_general(tau[0, at, :], stack[...], dims, preferred_element_type=F32)
            total += lax.dot_general(tau[1, at, :], stack2[...], dims, preferred_element_type=F32)
            total = total.reshape(owners, 2, half, 2 * rows + pad)
            blank = jnp.zeros((owners * half, span - 2 * rows - pad), F32)
            upper = jnp.concatenate([total[:, 0].reshape(owners * half, 2 * rows + pad), blank], axis=1)
            lower = jnp.concatenate([blank, total[:, 1].reshape(owners * half, 2 * rows + pad)], axis=1)
            packed = upper + pltpu.roll(lower, pad, 1)
            turned[o, pl.ds(i * owners, owners)] = packed.astype(BF16).reshape(owners, half, span)

            @pl.loop(0, owners)
            def _(step):
                to = i * owners + (mode + step) % owners

                @pl.when(to != mode)
                def _():
                    slab(o, to, mode).start()

        own_slab(o).start()

    wide = 768

    def sink_product(o):
        wait_stage3(o, 0)
        left[pl.ds(0, rows), pl.ds(0, order)] = w_sink[o, 0]
        left[pl.ds(0, rows), pl.ds(order, order)] = -w_sink[o, 1]
        left[pl.ds(rows, rows), pl.ds(0, order)] = w_sink[o, 1]
        left[pl.ds(rows, rows), pl.ds(order, order)] = w_sink[o, 0]

        @pl.loop(0, order // wide)
        def _(i):
            at = pl.ds(pl.multiple_of(i * wide, 128), wide)
            total = jnp.dot(left[...], tau[:, :, at].reshape(2 * order, wide), preferred_element_type=F32)
            sink[o, :, :, at] = total.astype(BF16).reshape(2, rows, wide)

    tall = 16

    def align(o, then=None, start=()):
        group = lax.broadcasted_iota(jnp.int32, (tall, span), 1) // rows
        picks = [group == b for b in range(3)]
        own_slab(o).wait()

        def from_group(step, sums):
            g = (mode // 4 + step) % 4

            @pl.loop(4 * g, 4 * g + 4)
            def _(sender):
                @pl.when(sender != mode)
                def _():
                    slab(o, sender, sender).wait_recv()

            @pl.loop(0, half // tall)
            def _(it):
                row = pl.ds(pl.multiple_of(it * tall, tall), tall)
                blocks = [arrived[o, 4 * g + b, row, :].astype(F32) for b in range(4)]
                for a in range(4):
                    moved = [
                        blocks[b] if a == b else pltpu.roll(blocks[b], (rows * (b - a)) % span, 1)
                        for b in range(4)
                    ]
                    part = jnp.where(
                        picks[0], moved[0], jnp.where(picks[1], moved[1], jnp.where(picks[2], moved[2], moved[3])))
                    down_to = pl.ds(pl.multiple_of((a // 2) * half + it * tall, tall), tall)
                    aligned[o, a % 2, down_to, pl.ds(pl.multiple_of(g * span, 128), span)] = part.astype(BF16)

            return sums if then is None else then(g, sums)

        return lax.fori_loop(0, MODES // 4, from_group, start)

    def terms(os, qs, at, sums):
        wide = at.size

        def body(it, sums):
            sums = list(sums)
            row = pl.ds(pl.multiple_of(it * tall, tall), tall)
            right = [(aligned[q, 0, row, at].astype(F32), aligned[q, 1, row, at].astype(F32)) for q in qs]
            k = 0
            for o in os:
                s_re, s_im = sink[o, 0, row, at].astype(F32), sink[o, 1, row, at].astype(F32)
                for t_re, t_im in right:
                    for value in (s_re * t_re + s_im * t_im, s_im * t_re - s_re * t_im):
                        value = value[:8] + value[8:]
                        for lanes in range(0, wide, 128):
                            sums[k] += value[:, lanes:lanes + 128]
                        k += 1
            return tuple(sums)

        return lax.fori_loop(0, rows // tall, body, sums)

    def blank_sums(os, qs):
        return (jnp.zeros((8, 128), F32),) * (2 * len(os) * len(qs))

    def keep(os, qs, sums):
        k = 0
        for o in os:
            for q in qs:
                for part in range(2):
                    index = q * 2 * OPS + 2 * o + part
                    lines[index:index + 1, :] = jnp.sum(sums[k], axis=0, keepdims=True)
                    k += 1

    def contract(os, qs):
        def body(it, sums):
            return terms(os, qs, pl.ds(pl.multiple_of(it * 256, 128), 256), sums)

        keep(os, qs, lax.fori_loop(0, order // 256, body, blank_sums(os, qs)))

    def align_and_contract(o, os):
        def then(g, sums):
            return terms(os, (o,), pl.ds(pl.multiple_of(g * span, 128), span), sums)

        keep(os, (o,), align(o, then, blank_sums(os, (o,))))

    source(0)
    sink_product(0)
    source(1)
    stage3(3)
    sink_product(1)
    source(2)
    align(0)
    sink_product(2)
    source(3)
    align(1)
    sink_product(3)
    contract((0, 1, 2, 3), (0, 1))
    align(2)
    contract((0, 1, 2, 3), (2,))
    align_and_contract(3, (0, 1, 2, 3))

    column = jnp.sum(lines[...], axis=1, keepdims=True)
    lane = lax.broadcasted_iota(jnp.int32, (2 * OPS, 128), 1)
    tile = jnp.zeros((2 * OPS, 128), F32)
    for q in range(OPS):
        tile = jnp.where(lane == q, column[2 * OPS * q:2 * OPS * (q + 1)], tile)
    parts[mode] = tile

    @pl.loop(1, MODES)
    def _(step):
        remote(parts.at[mode], parts.at[mode], ps_send.at[step], ps_recv.at[step],
               (pair, (mode + step) % MODES)).start()

    @pl.loop(1, MODES)
    def _(step):
        remote(parts.at[mode], parts.at[mode], ps_send.at[step], ps_recv.at[step],
               (pair, (mode + step) % MODES)).wait()

    total = parts[0]
    for n in range(1, MODES):
        total = total + parts[n]
    total = total * (1.0 / order)
    for o in range(OPS):
        corr_ref[0, o] = total[2 * o:2 * o + 2, :OPS]

    for copy in want_copies:
        copy.wait_send()
    for copies, _ in first:
        for copy in copies:
            copy.wait_send()
    for copy in across:
        copy.wait_send()
    for copy in second.values():
        copy.wait_send()
    for copy in tau_copies.values():
        copy.wait_send()
    for o in range(OPS):
        @pl.loop(0, MODES)
        def _(to):
            @pl.when(to != mode)
            def _():
                slab(o, to, mode).wait_send()


def body(time_pairs, slot_of, elementals, propagators):
    _, ops, parts, rows, order = elementals.shape
    slots = slot_of.shape[0]
    quarter = order // XS
    dma = pltpu.SemaphoreType.DMA
    sink, corr = pl.pallas_call(
        kernel,
        out_shape=(
            pltpu.VMEM(elementals.shape, BF16),
            pltpu.VMEM((1, ops, 2, ops), F32),
        ),
        in_specs=[
            pl.BlockSpec(memory_space=pl.ANY),
            pl.BlockSpec(memory_space=pl.ANY),
            pl.BlockSpec(memory_space=pl.ANY),
            pl.BlockSpec(memory_space=pl.ANY),
        ],
        out_specs=(pl.BlockSpec(memory_space=pltpu.VMEM), pl.BlockSpec(memory_space=pltpu.VMEM)),
        scratch_shapes=[
            *[pltpu.VMEM((slots, 2, rows, quarter), BF16)] * OPS,
            pltpu.VMEM((ops, 2, XS - 1, 2, rows, quarter), BF16),
            pltpu.VMEM((ops, 2, rows, order), BF16),
            pltpu.VMEM((ops, 2, rows, order), BF16),
            pltpu.VMEM((2, order, order), BF16),
            pltpu.VMEM((256, order), BF16),
            pltpu.VMEM((256, order), BF16),
            pltpu.VMEM((2 * rows, 2 * order), BF16),
            pltpu.VMEM((ops, MODES, rows // 2, 4 * rows), BF16),
            pltpu.VMEM((ops, MODES, rows // 2, 4 * rows), BF16),
            pltpu.VMEM((ops, 2, rows, order), BF16),
            pltpu.SMEM(time_pairs.shape, jnp.int32),
            pltpu.SMEM(slot_of.shape, jnp.int32),
            pltpu.VMEM((XS, 8, 128), jnp.int32),
            pltpu.SMEM((XS, 8, 128), jnp.int32),
            pltpu.VMEM((ops * ops * 2, 128), F32),
            pltpu.VMEM((MODES, 2 * ops, 128), F32),
            dma((XS - 1,)), dma((XS - 1,)),
            dma((OPS, XS - 1)), dma((OPS, XS - 1)),
            dma((OPS,)), dma((OPS,)),
            dma((OPS, 2, XS - 1)), dma((OPS, 2, XS - 1)),
            dma((24,)), dma((24,)),
            dma((OPS, MODES)), dma((OPS, MODES)),
            dma((MODES,)), dma((MODES,)),
            dma((3 + OPS + OPS,)),
        ],
        compiler_params=pltpu.CompilerParams(
            collective_id=0, has_side_effects=True, vmem_limit_bytes=56 << 20
        ),
        name="meson",
    )(time_pairs, slot_of, elementals, propagators)
    return jnp.swapaxes(corr, 2, 3), sink


def solution(mesh):
    in_specs = (
        P("pair", None),
        P(),
        P("pair", None, None, "mode", None),
        P("pair", None, "mode", None),
    )
    out_specs = (P("pair", None, None, None), P("pair", None, None, "mode", None))
    return jax.shard_map(body, mesh=mesh, in_specs=in_specs, out_specs=out_specs, check_vma=False)
```

```python
import jax
import jax.numpy as jnp
from jax import lax
from jax.experimental import pallas as pl
from jax.experimental.pallas import tpu as pltpu
from jax.sharding import PartitionSpec as P

MESH = pl.DeviceIdType.MESH
F32 = jnp.float32
BF16 = jnp.bfloat16
XS = 4
MODES = 16
OPS = 4
SLOTS = 8


def kernel(times_ref, slots_ref, elem_ref, prop_ref, sink_ref, corr_ref,
           r0, r1, r2, r3, staged, w_sink, w_source, tau, stack, stack2, left, turned, arrived, aligned,
           times, slots, want_all, want_smem, lines, parts,
           want_send, want_recv, p1_send, p1_recv, y_send, y_recv, p2_send, p2_recv,
           tau_send, tau_recv, t_send, t_recv, ps_send, ps_recv, local):
    elem, prop, sink = elem_ref.at[0], prop_ref.at[0], sink_ref.at[0]
    rows = elem.shape[2]
    order = elem.shape[3]
    quarter = order // XS
    gathered = (r0, r1, r2, r3)

    pair = lax.axis_index("pair")
    mode = lax.axis_index("mode")
    yh, x = pair // XS, pair % XS
    yl, z, core = mode // 8, (mode // 2) % 4, mode % 2

    def at_x(step):
        return (yh * XS + (x + step) % XS, mode)

    y_partner = ((1 - yh) * XS + x, mode)

    def chunk(y_at, z_at, core_at):
        return y_at * 8 + z_at * 2 + core_at

    def at_mode(y_at, z_at, core_at):
        return (pair, chunk(y_at, z_at, core_at))

    def remote(src, dst, send, recv, device):
        return pltpu.make_async_remote_copy(
            src_ref=src, dst_ref=dst, send_sem=send, recv_sem=recv,
            device_id=device, device_id_type=MESH)

    load_times = pltpu.make_async_copy(times_ref, times, local.at[0])
    load_slots = pltpu.make_async_copy(slots_ref, slots, local.at[2 + 2 * OPS])
    load_times.start()
    load_slots.start()

    barrier = pltpu.get_barrier_semaphore()
    for step in range(1, XS):
        pl.semaphore_signal(barrier, inc=1, device_id=at_x(step), device_id_type=MESH)
    pl.semaphore_signal(barrier, inc=1, device_id=y_partner, device_id_type=MESH)

    @pl.loop(1, MODES)
    def _(step):
        pl.semaphore_signal(barrier, inc=1, device_id=(pair, (mode + step) % MODES), device_id_type=MESH)

    pl.semaphore_wait(barrier, XS - 1 + 1 + MODES - 1)

    def columns(at):
        return pl.ds(pl.multiple_of(at * quarter, 128), quarter)

    def stage1(o):
        copies = []
        for s in (2, 1, 3):
            copies.append(remote(
                elem.at[o, :, :, columns((x + s) % XS)], gathered[o].at[pair],
                p1_send.at[o, s - 1], p1_recv.at[o, s - 1], at_x(s)))
        own = pltpu.make_async_copy(elem.at[o, :, :, columns(x)], gathered[o].at[pair], local.at[1 + o])
        return copies, own

    first = [stage1(o) for o in range(OPS)]

    half = rows // 2
    tau_copies = {}

    def tau_rows(index, start=0, size=rows):
        return tau.at[:, pl.ds(pl.multiple_of(index * rows + start, 16), size), :]

    def pass_on(name, src, dst, device):
        k = len(tau_copies)
        copy = remote(src, dst, tau_send.at[k], tau_recv.at[k], device)
        copy.start()
        tau_copies[name] = copy

    def pass_rows(name, index, device, start=0, size=rows):
        ref = tau_rows(index, start, size)
        pass_on(name, ref, ref, device)

    zp, zm, zf = (z + 1) % 4, (z + 3) % 4, (z + 2) % 4
    up, down, sibling = at_mode(yl, zp, core), at_mode(yl, zm, core), at_mode(yl, z, 1 - core)
    own_chunk = chunk(yl, z, core)

    pass_on("y", prop, tau_rows(own_chunk), at_mode(1 - yl, z, core))
    for copy in first[0][0]:
        copy.start()
    first[0][1].start()
    pass_on("z+", prop, tau_rows(own_chunk), up)
    pass_on("z-", prop, tau_rows(own_chunk), down)
    pass_on("c", prop, tau_rows(own_chunk), sibling)
    own_tau = pltpu.make_async_copy(prop, tau_rows(own_chunk), local.at[1 + OPS])
    own_tau.start()
    for copy in first[1][0]:
        copy.start()
    first[1][1].start()

    load_times.wait()
    load_slots.wait()
    line = lax.broadcasted_iota(jnp.int32, (8, 128), 0)
    want_all[x] = jnp.where(line == 0, slots[times[0, 0]], slots[times[0, 1]])
    want_copies = [
        remote(want_all.at[x], want_all.at[x], want_send.at[s - 1], want_recv.at[s - 1], at_x(s))
        for s in range(1, XS)
    ]
    for copy in want_copies:
        copy.start()
    for o in range(2, OPS):
        for copy in first[o][0]:
            copy.start()
        first[o][1].start()

    plane = pl.ds(yh * XS, XS)
    across = [
        remote(gathered[o].at[plane], gathered[o].at[plane], y_send.at[o], y_recv.at[o], y_partner)
        for o in range(OPS)
    ]

    def stage2(o):
        copies, own = first[o]
        own.wait()
        for copy in copies:
            copy.wait_recv()
        across[o].start()

    second = {}

    def stage3(o):
        across[o].wait_recv()
        for k, held in ((1, w_source), (0, w_sink)):
            for s in (2, 1, 3):
                slot = want_smem[(x + s) % XS, k, 0]
                staged[o, k, s - 1] = gathered[o][slot]
                copy = remote(
                    staged.at[o, k, s - 1], held.at[o, :, :, columns(x)],
                    p2_send.at[o, k, s - 1], p2_recv.at[o, k, s - 1], at_x(s))
                copy.start()
                second[o, k, s] = copy
            held[o, :, :, columns(x)] = gathered[o][want_smem[x, k, 0]]

    def wait_stage3(o, k):
        for s in range(1, XS):
            second[o, k, s].wait_recv()

    def relay(letter, y_at):
        tau_copies[letter + "z+"].wait_recv()
        below = chunk(y_at, zm, core)
        pass_rows(letter + "h+", below, up, 0, half)
        pass_rows(letter + "cz+", below, sibling)
        tau_copies[letter + "z-"].wait_recv()
        above = chunk(y_at, zp, core)
        pass_rows(letter + "h-", above, down, half, half)
        pass_rows(letter + "cz-", above, sibling)

    def relay_far(letter, y_at):
        far = chunk(y_at, zf, core)
        tau_copies[letter + "h+"].wait_recv()
        pass_rows(letter + "ch+", far, sibling, 0, half)
        tau_copies[letter + "h-"].wait_recv()
        pass_rows(letter + "ch-", far, sibling, half, half)

    stage2(0)
    for copy in want_copies:
        copy.wait_recv()
    to_smem = pltpu.make_async_copy(want_all, want_smem, local.at[0])
    to_smem.start()
    stage2(1)
    tau_copies["y"].wait_recv()
    other = chunk(1 - yl, z, core)
    pass_rows("Vz+", other, up)
    pass_rows("Vz-", other, down)
    pass_rows("Vc", other, sibling)
    relay("", yl)
    stage2(2)
    to_smem.wait()
    stage3(0)
    relay_far("", yl)
    stage2(3)
    relay("V", 1 - yl)
    stage3(1)
    relay_far("V", 1 - yl)
    stage3(2)
    own_tau.wait()
    for name in ("c", "Vc", "cz+", "cz-", "Vcz+", "Vcz-", "ch+", "ch-", "Vch+", "Vch-"):
        tau_copies[name].wait_recv()

    span = 4 * rows
    dims = (((1,), (1,)), ((), ()))
    pad = stack.shape[0] - 2 * rows
    stack[pl.ds(2 * rows, pad), :] = jnp.zeros((pad, order), BF16)
    stack2[pl.ds(2 * rows, pad), :] = jnp.zeros((pad, order), BF16)

    def slab(o, to, sender):
        return remote(turned.at[o, to], arrived.at[o, sender], t_send.at[o, to], t_recv.at[o, sender], (pair, to))

    def own_slab(o):
        return pltpu.make_async_copy(turned.at[o, mode], arrived.at[o, mode], local.at[2 + OPS + o])

    def source(o):
        wait_stage3(o, 1)
        real, imag = w_source[o, 0], w_source[o, 1]
        stack[pl.ds(0, rows), :] = real
        stack[pl.ds(rows, rows), :] = -imag
        stack2[pl.ds(0, rows), :] = imag
        stack2[pl.ds(rows, rows), :] = real

        blocks = 2
        many = order // blocks
        owners = MODES // blocks

        @pl.loop(0, blocks)
        def _(count):
            i = (1 - yl + count) % 2
            at = pl.ds(pl.multiple_of(i * many, 16), many)
            total = lax.dot_general(tau[0, at, :], stack[...], dims, preferred_element_type=F32)
            total += lax.dot_general(tau[1, at, :], stack2[...], dims, preferred_element_type=F32)
            total = total.reshape(owners, 2, half, 2 * rows + pad)
            blank = jnp.zeros((owners * half, span - 2 * rows - pad), F32)
            upper = jnp.concatenate([total[:, 0].reshape(owners * half, 2 * rows + pad), blank], axis=1)
            lower = jnp.concatenate([blank, total[:, 1].reshape(owners * half, 2 * rows + pad)], axis=1)
            packed = upper + pltpu.roll(lower, pad, 1)
            turned[o, pl.ds(i * owners, owners)] = packed.astype(BF16).reshape(owners, half, span)

            @pl.loop(0, owners)
            def _(step):
                to = i * owners + (mode + step) % owners

                @pl.when(to != mode)
                def _():
                    slab(o, to, mode).start()

        own_slab(o).start()

    wide = 768

    def sink_product(o):
        wait_stage3(o, 0)
        left[pl.ds(0, rows), pl.ds(0, order)] = w_sink[o, 0]
        left[pl.ds(0, rows), pl.ds(order, order)] = -w_sink[o, 1]
        left[pl.ds(rows, rows), pl.ds(0, order)] = w_sink[o, 1]
        left[pl.ds(rows, rows), pl.ds(order, order)] = w_sink[o, 0]

        @pl.loop(0, order // wide)
        def _(i):
            at = pl.ds(pl.multiple_of(i * wide, 128), wide)
            total = jnp.dot(left[...], tau[:, :, at].reshape(2 * order, wide), preferred_element_type=F32)
            sink[o, :, :, at] = total.astype(BF16).reshape(2, rows, wide)

    tall = 16

    def align(o, then=None, start=()):
        group = lax.broadcasted_iota(jnp.int32, (tall, span), 1) // rows
        picks = [group == b for b in range(3)]
        own_slab(o).wait()

        def from_group(step, sums):
            g = (mode // 4 + step) % 4

            @pl.loop(4 * g, 4 * g + 4)
            def _(sender):
                @pl.when(sender != mode)
                def _():
                    slab(o, sender, sender).wait_recv()

            @pl.loop(0, half // tall)
            def _(it):
                row = pl.ds(pl.multiple_of(it * tall, tall), tall)
                blocks = [arrived[o, 4 * g + b, row, :].astype(F32) for b in range(4)]
                for a in range(4):
                    moved = [
                        blocks[b] if a == b else pltpu.roll(blocks[b], (rows * (b - a)) % span, 1)
                        for b in range(4)
                    ]
                    part = jnp.where(
                        picks[0], moved[0], jnp.where(picks[1], moved[1], jnp.where(picks[2], moved[2], moved[3])))
                    down_to = pl.ds(pl.multiple_of((a // 2) * half + it * tall, tall), tall)
                    aligned[o, a % 2, down_to, pl.ds(pl.multiple_of(g * span, 128), span)] = part.astype(BF16)

            return sums if then is None else then(g, sums)

        return lax.fori_loop(0, MODES // 4, from_group, start)

    def terms(os, qs, at, sums):
        wide = at.size

        def body(it, sums):
            sums = list(sums)
            row = pl.ds(pl.multiple_of(it * tall, tall), tall)
            right = [(aligned[q, 0, row, at].astype(F32), aligned[q, 1, row, at].astype(F32)) for q in qs]
            k = 0
            for o in os:
                s_re, s_im = sink[o, 0, row, at].astype(F32), sink[o, 1, row, at].astype(F32)
                for t_re, t_im in right:
                    for value in (s_re * t_re + s_im * t_im, s_im * t_re - s_re * t_im):
                        value = value[:8] + value[8:]
                        for lanes in range(0, wide, 128):
                            sums[k] += value[:, lanes:lanes + 128]
                        k += 1
            return tuple(sums)

        return lax.fori_loop(0, rows // tall, body, sums)

    def blank_sums(os, qs):
        return (jnp.zeros((8, 128), F32),) * (2 * len(os) * len(qs))

    def keep(os, qs, sums):
        k = 0
        for o in os:
            for q in qs:
                for part in range(2):
                    index = q * 2 * OPS + 2 * o + part
                    lines[index:index + 1, :] = jnp.sum(sums[k], axis=0, keepdims=True)
                    k += 1

    def contract(os, qs):
        def body(it, sums):
            return terms(os, qs, pl.ds(pl.multiple_of(it * 256, 128), 256), sums)

        keep(os, qs, lax.fori_loop(0, order // 256, body, blank_sums(os, qs)))

    def align_and_contract(o, os):
        def then(g, sums):
            return terms(os, (o,), pl.ds(pl.multiple_of(g * span, 128), span), sums)

        keep(os, (o,), align(o, then, blank_sums(os, (o,))))

    source(0)
    sink_product(0)
    source(1)
    stage3(3)
    sink_product(1)
    source(2)
    align(0)
    sink_product(2)
    source(3)
    align(1)
    sink_product(3)
    contract((0, 1, 2, 3), (0, 1))
    align(2)
    contract((0, 1, 2, 3), (2,))

    for copy in want_copies:
        copy.wait_send()
    for copies, _ in first:
        for copy in copies:
            copy.wait_send()
    for copy in across:
        copy.wait_send()
    for copy in second.values():
        copy.wait_send()
    for copy in tau_copies.values():
        copy.wait_send()

    def slabs_left(o):
        @pl.loop(0, MODES)
        def _(to):
            @pl.when(to != mode)
            def _():
                slab(o, to, mode).wait_send()

    slabs_left(0)
    slabs_left(1)
    align_and_contract(3, (0, 1, 2, 3))

    column = jnp.sum(lines[...], axis=1, keepdims=True)
    lane = lax.broadcasted_iota(jnp.int32, (2 * OPS, 128), 1)
    tile = jnp.zeros((2 * OPS, 128), F32)
    for q in range(OPS):
        tile = jnp.where(lane == q, column[2 * OPS * q:2 * OPS * (q + 1)], tile)
    parts[mode] = tile

    @pl.loop(1, MODES)
    def _(step):
        remote(parts.at[mode], parts.at[mode], ps_send.at[step], ps_recv.at[step],
               (pair, (mode + step) % MODES)).start()

    slabs_left(2)
    slabs_left(3)

    @pl.loop(1, MODES)
    def _(step):
        remote(parts.at[mode], parts.at[mode], ps_send.at[step], ps_recv.at[step],
               (pair, (mode + step) % MODES)).wait()

    total = parts[0]
    for n in range(1, MODES):
        total = total + parts[n]
    total = total * (1.0 / order)
    for o in range(OPS):
        corr_ref[0, o] = total[2 * o:2 * o + 2, :OPS]


def body(time_pairs, slot_of, elementals, propagators):
    _, ops, parts, rows, order = elementals.shape
    slots = slot_of.shape[0]
    quarter = order // XS
    dma = pltpu.SemaphoreType.DMA
    sink, corr = pl.pallas_call(
        kernel,
        out_shape=(
            pltpu.VMEM(elementals.shape, BF16),
            pltpu.VMEM((1, ops, 2, ops), F32),
        ),
        in_specs=[
            pl.BlockSpec(memory_space=pl.ANY),
            pl.BlockSpec(memory_space=pl.ANY),
            pl.BlockSpec(memory_space=pl.ANY),
            pl.BlockSpec(memory_space=pl.ANY),
        ],
        out_specs=(pl.BlockSpec(memory_space=pltpu.VMEM), pl.BlockSpec(memory_space=pltpu.VMEM)),
        scratch_shapes=[
            *[pltpu.VMEM((slots, 2, rows, quarter), BF16)] * OPS,
            pltpu.VMEM((ops, 2, XS - 1, 2, rows, quarter), BF16),
            pltpu.VMEM((ops, 2, rows, order), BF16),
            pltpu.VMEM((ops, 2, rows, order), BF16),
            pltpu.VMEM((2, order, order), BF16),
            pltpu.VMEM((256, order), BF16),
            pltpu.VMEM((256, order), BF16),
            pltpu.VMEM((2 * rows, 2 * order), BF16),
            pltpu.VMEM((ops, MODES, rows // 2, 4 * rows), BF16),
            pltpu.VMEM((ops, MODES, rows // 2, 4 * rows), BF16),
            pltpu.VMEM((ops, 2, rows, order), BF16),
            pltpu.SMEM(time_pairs.shape, jnp.int32),
            pltpu.SMEM(slot_of.shape, jnp.int32),
            pltpu.VMEM((XS, 8, 128), jnp.int32),
            pltpu.SMEM((XS, 8, 128), jnp.int32),
            pltpu.VMEM((ops * ops * 2, 128), F32),
            pltpu.VMEM((MODES, 2 * ops, 128), F32),
            dma((XS - 1,)), dma((XS - 1,)),
            dma((OPS, XS - 1)), dma((OPS, XS - 1)),
            dma((OPS,)), dma((OPS,)),
            dma((OPS, 2, XS - 1)), dma((OPS, 2, XS - 1)),
            dma((24,)), dma((24,)),
            dma((OPS, MODES)), dma((OPS, MODES)),
            dma((MODES,)), dma((MODES,)),
            dma((3 + OPS + OPS,)),
        ],
        compiler_params=pltpu.CompilerParams(
            collective_id=0, has_side_effects=True, vmem_limit_bytes=56 << 20
        ),
        name="meson",
    )(time_pairs, slot_of, elementals, propagators)
    return jnp.swapaxes(corr, 2, 3), sink


def solution(mesh):
    in_specs = (
        P("pair", None),
        P(),
        P("pair", None, None, "mode", None),
        P("pair", None, "mode", None),
    )
    out_specs = (P("pair", None, None, None), P("pair", None, None, "mode", None))
    return jax.shard_map(body, mesh=mesh, in_specs=in_specs, out_specs=out_specs, check_vma=False)
```

```python
import jax
import jax.numpy as jnp
from jax import lax
from jax.experimental import pallas as pl
from jax.experimental.pallas import tpu as pltpu
from jax.sharding import PartitionSpec as P

MESH = pl.DeviceIdType.MESH
F32 = jnp.float32
BF16 = jnp.bfloat16
XS = 4
MODES = 16
OPS = 4
SLOTS = 8


def kernel(times_ref, slots_ref, elem_ref, prop_ref, sink_ref, corr_ref,
           r0, r1, r2, r3, staged, w_sink, w_source, tau, stack, stack2, left, turned, arrived, aligned,
           times, slots, want_all, want_smem, lines, parts,
           want_send, want_recv, p1_send, p1_recv, y_send, y_recv, p2_send, p2_recv,
           tau_send, tau_recv, t_send, t_recv, ps_send, ps_recv, local):
    elem, prop, sink = elem_ref.at[0], prop_ref.at[0], sink_ref.at[0]
    rows = elem.shape[2]
    order = elem.shape[3]
    quarter = order // XS
    gathered = (r0, r1, r2, r3)

    pair = lax.axis_index("pair")
    mode = lax.axis_index("mode")
    yh, x = pair // XS, pair % XS
    yl, z, core = mode // 8, (mode // 2) % 4, mode % 2

    def at_x(step):
        return (yh * XS + (x + step) % XS, mode)

    y_partner = ((1 - yh) * XS + x, mode)

    def chunk(y_at, z_at, core_at):
        return y_at * 8 + z_at * 2 + core_at

    def at_mode(y_at, z_at, core_at):
        return (pair, chunk(y_at, z_at, core_at))

    def remote(src, dst, send, recv, device):
        return pltpu.make_async_remote_copy(
            src_ref=src, dst_ref=dst, send_sem=send, recv_sem=recv,
            device_id=device, device_id_type=MESH)

    load_times = pltpu.make_async_copy(times_ref, times, local.at[0])
    load_slots = pltpu.make_async_copy(slots_ref, slots, local.at[2 + 2 * OPS])
    load_times.start()
    load_slots.start()

    barrier = pltpu.get_barrier_semaphore()
    for step in range(1, XS):
        pl.semaphore_signal(barrier, inc=1, device_id=at_x(step), device_id_type=MESH)
    pl.semaphore_signal(barrier, inc=1, device_id=y_partner, device_id_type=MESH)

    @pl.loop(1, MODES)
    def _(step):
        pl.semaphore_signal(barrier, inc=1, device_id=(pair, (mode + step) % MODES), device_id_type=MESH)

    pl.semaphore_wait(barrier, XS - 1 + 1 + MODES - 1)

    def columns(at):
        return pl.ds(pl.multiple_of(at * quarter, 128), quarter)

    def stage1(o):
        copies = []
        for s in (2, 1, 3):
            copies.append(remote(
                elem.at[o, :, :, columns((x + s) % XS)], gathered[o].at[pair],
                p1_send.at[o, s - 1], p1_recv.at[o, s - 1], at_x(s)))
        own = pltpu.make_async_copy(elem.at[o, :, :, columns(x)], gathered[o].at[pair], local.at[1 + o])
        return copies, own

    first = [stage1(o) for o in range(OPS)]

    half = rows // 2
    tau_copies = {}

    def tau_rows(index, start=0, size=rows):
        return tau.at[:, pl.ds(pl.multiple_of(index * rows + start, 16), size), :]

    def pass_on(name, src, dst, device):
        k = len(tau_copies)
        copy = remote(src, dst, tau_send.at[k], tau_recv.at[k], device)
        copy.start()
        tau_copies[name] = copy

    def pass_rows(name, index, device, start=0, size=rows):
        ref = tau_rows(index, start, size)
        pass_on(name, ref, ref, device)

    zp, zm, zf = (z + 1) % 4, (z + 3) % 4, (z + 2) % 4
    up, down, sibling = at_mode(yl, zp, core), at_mode(yl, zm, core), at_mode(yl, z, 1 - core)
    own_chunk = chunk(yl, z, core)

    pass_on("y", prop, tau_rows(own_chunk), at_mode(1 - yl, z, core))
    for copy in first[0][0]:
        copy.start()
    first[0][1].start()
    pass_on("z+", prop, tau_rows(own_chunk), up)
    pass_on("z-", prop, tau_rows(own_chunk), down)
    pass_on("c", prop, tau_rows(own_chunk), sibling)
    own_tau = pltpu.make_async_copy(prop, tau_rows(own_chunk), local.at[1 + OPS])
    own_tau.start()
    for copy in first[1][0]:
        copy.start()
    first[1][1].start()

    load_times.wait()
    load_slots.wait()
    line = lax.broadcasted_iota(jnp.int32, (8, 128), 0)
    want_all[x] = jnp.where(line == 0, slots[times[0, 0]], slots[times[0, 1]])
    want_copies = [
        remote(want_all.at[x], want_all.at[x], want_send.at[s - 1], want_recv.at[s - 1], at_x(s))
        for s in range(1, XS)
    ]
    for copy in want_copies:
        copy.start()

    plane = pl.ds(yh * XS, XS)
    across = [
        remote(gathered[o].at[plane], gathered[o].at[plane], y_send.at[o], y_recv.at[o], y_partner)
        for o in range(OPS)
    ]

    def stage2(o):
        copies, own = first[o]
        own.wait()
        for copy in copies:
            copy.wait_recv()
        across[o].start()
        if o + 2 < OPS:
            for copy in first[o + 2][0]:
                copy.start()
            first[o + 2][1].start()

    second = {}

    def stage3(o):
        across[o].wait_recv()
        for k, held in ((1, w_source), (0, w_sink)):
            for s in (2, 1, 3):
                slot = want_smem[(x + s) % XS, k, 0]
                staged[o, k, s - 1] = gathered[o][slot]
                copy = remote(
                    staged.at[o, k, s - 1], held.at[o, :, :, columns(x)],
                    p2_send.at[o, k, s - 1], p2_recv.at[o, k, s - 1], at_x(s))
                copy.start()
                second[o, k, s] = copy
            held[o, :, :, columns(x)] = gathered[o][want_smem[x, k, 0]]

    def wait_stage3(o, k):
        for s in range(1, XS):
            second[o, k, s].wait_recv()

    def relay(letter, y_at):
        tau_copies[letter + "z+"].wait_recv()
        below = chunk(y_at, zm, core)
        pass_rows(letter + "h+", below, up, 0, half)
        pass_rows(letter + "cz+", below, sibling)
        tau_copies[letter + "z-"].wait_recv()
        above = chunk(y_at, zp, core)
        pass_rows(letter + "h-", above, down, half, half)
        pass_rows(letter + "cz-", above, sibling)

    def relay_far(letter, y_at):
        far = chunk(y_at, zf, core)
        tau_copies[letter + "h+"].wait_recv()
        pass_rows(letter + "ch+", far, sibling, 0, half)
        tau_copies[letter + "h-"].wait_recv()
        pass_rows(letter + "ch-", far, sibling, half, half)

    stage2(0)
    for copy in want_copies:
        copy.wait_recv()
    to_smem = pltpu.make_async_copy(want_all, want_smem, local.at[0])
    to_smem.start()
    stage2(1)
    tau_copies["y"].wait_recv()
    other = chunk(1 - yl, z, core)
    pass_rows("Vz+", other, up)
    pass_rows("Vz-", other, down)
    pass_rows("Vc", other, sibling)
    relay("", yl)
    stage2(2)
    to_smem.wait()
    stage3(0)
    relay_far("", yl)
    stage2(3)
    relay("V", 1 - yl)
    stage3(1)
    relay_far("V", 1 - yl)
    stage3(2)
    own_tau.wait()
    for name in ("c", "Vc", "cz+", "cz-", "Vcz+", "Vcz-", "ch+", "ch-", "Vch+", "Vch-"):
        tau_copies[name].wait_recv()

    span = 4 * rows
    dims = (((1,), (1,)), ((), ()))
    pad = stack.shape[0] - 2 * rows
    stack[pl.ds(2 * rows, pad), :] = jnp.zeros((pad, order), BF16)
    stack2[pl.ds(2 * rows, pad), :] = jnp.zeros((pad, order), BF16)

    def slab(o, to, sender):
        return remote(turned.at[o, to], arrived.at[o, sender], t_send.at[o, to], t_recv.at[o, sender], (pair, to))

    def own_slab(o):
        return pltpu.make_async_copy(turned.at[o, mode], arrived.at[o, mode], local.at[2 + OPS + o])

    def source(o):
        wait_stage3(o, 1)
        real, imag = w_source[o, 0], w_source[o, 1]
        stack[pl.ds(0, rows), :] = real
        stack[pl.ds(rows, rows), :] = -imag
        stack2[pl.ds(0, rows), :] = imag
        stack2[pl.ds(rows, rows), :] = real

        blocks = 2
        many = order // blocks
        owners = MODES // blocks

        @pl.loop(0, blocks)
        def _(count):
            i = (1 - yl + count) % 2
            at = pl.ds(pl.multiple_of(i * many, 16), many)
            total = lax.dot_general(tau[0, at, :], stack[...], dims, preferred_element_type=F32)
            total += lax.dot_general(tau[1, at, :], stack2[...], dims, preferred_element_type=F32)
            total = total.reshape(owners, 2, half, 2 * rows + pad)
            blank = jnp.zeros((owners * half, span - 2 * rows - pad), F32)
            upper = jnp.concatenate([total[:, 0].reshape(owners * half, 2 * rows + pad), blank], axis=1)
            lower = jnp.concatenate([blank, total[:, 1].reshape(owners * half, 2 * rows + pad)], axis=1)
            packed = upper + pltpu.roll(lower, pad, 1)
            turned[o, pl.ds(i * owners, owners)] = packed.astype(BF16).reshape(owners, half, span)

            @pl.loop(0, owners)
            def _(step):
                to = i * owners + (mode + step) % owners

                @pl.when(to != mode)
                def _():
                    slab(o, to, mode).start()

        own_slab(o).start()

    wide = 768

    def sink_product(o):
        wait_stage3(o, 0)
        left[pl.ds(0, rows), pl.ds(0, order)] = w_sink[o, 0]
        left[pl.ds(0, rows), pl.ds(order, order)] = -w_sink[o, 1]
        left[pl.ds(rows, rows), pl.ds(0, order)] = w_sink[o, 1]
        left[pl.ds(rows, rows), pl.ds(order, order)] = w_sink[o, 0]

        @pl.loop(0, order // wide)
        def _(i):
            at = pl.ds(pl.multiple_of(i * wide, 128), wide)
            total = jnp.dot(left[...], tau[:, :, at].reshape(2 * order, wide), preferred_element_type=F32)
            sink[o, :, :, at] = total.astype(BF16).reshape(2, rows, wide)

    tall = 16

    def align(o, then=None, start=()):
        group = lax.broadcasted_iota(jnp.int32, (tall, span), 1) // rows
        picks = [group == b for b in range(3)]
        own_slab(o).wait()

        def from_group(step, sums):
            g = (mode // 4 + step) % 4

            @pl.loop(4 * g, 4 * g + 4)
            def _(sender):
                @pl.when(sender != mode)
                def _():
                    slab(o, sender, sender).wait_recv()

            @pl.loop(0, half // tall)
            def _(it):
                row = pl.ds(pl.multiple_of(it * tall, tall), tall)
                blocks = [arrived[o, 4 * g + b, row, :].astype(F32) for b in range(4)]
                for a in range(4):
                    moved = [
                        blocks[b] if a == b else pltpu.roll(blocks[b], (rows * (b - a)) % span, 1)
                        for b in range(4)
                    ]
                    part = jnp.where(
                        picks[0], moved[0], jnp.where(picks[1], moved[1], jnp.where(picks[2], moved[2], moved[3])))
                    down_to = pl.ds(pl.multiple_of((a // 2) * half + it * tall, tall), tall)
                    aligned[o, a % 2, down_to, pl.ds(pl.multiple_of(g * span, 128), span)] = part.astype(BF16)

            return sums if then is None else then(g, sums)

        return lax.fori_loop(0, MODES // 4, from_group, start)

    def terms(os, qs, at, sums):
        wide = at.size

        def body(it, sums):
            sums = list(sums)
            row = pl.ds(pl.multiple_of(it * tall, tall), tall)
            right = [(aligned[q, 0, row, at].astype(F32), aligned[q, 1, row, at].astype(F32)) for q in qs]
            k = 0
            for o in os:
                s_re, s_im = sink[o, 0, row, at].astype(F32), sink[o, 1, row, at].astype(F32)
                for t_re, t_im in right:
                    for value in (s_re * t_re + s_im * t_im, s_im * t_re - s_re * t_im):
                        value = value[:8] + value[8:]
                        for lanes in range(0, wide, 128):
                            sums[k] += value[:, lanes:lanes + 128]
                        k += 1
            return tuple(sums)

        return lax.fori_loop(0, rows // tall, body, sums)

    def blank_sums(os, qs):
        return (jnp.zeros((8, 128), F32),) * (2 * len(os) * len(qs))

    def keep(os, qs, sums):
        k = 0
        for o in os:
            for q in qs:
                for part in range(2):
                    index = q * 2 * OPS + 2 * o + part
                    lines[index:index + 1, :] = jnp.sum(sums[k], axis=0, keepdims=True)
                    k += 1

    def contract(os, qs):
        def body(it, sums):
            return terms(os, qs, pl.ds(pl.multiple_of(it * 256, 128), 256), sums)

        keep(os, qs, lax.fori_loop(0, order // 256, body, blank_sums(os, qs)))

    def align_and_contract(o, os):
        def then(g, sums):
            return terms(os, (o,), pl.ds(pl.multiple_of(g * span, 128), span), sums)

        keep(os, (o,), align(o, then, blank_sums(os, (o,))))

    source(0)
    sink_product(0)
    source(1)
    stage3(3)
    sink_product(1)
    source(2)
    align(0)
    sink_product(2)
    source(3)
    align(1)
    sink_product(3)
    contract((0, 1, 2, 3), (0, 1))
    align(2)
    contract((0, 1, 2, 3), (2,))

    for copy in want_copies:
        copy.wait_send()
    for copies, _ in first:
        for copy in copies:
            copy.wait_send()
    for copy in across:
        copy.wait_send()
    for copy in second.values():
        copy.wait_send()
    for copy in tau_copies.values():
        copy.wait_send()

    def slabs_left(o):
        @pl.loop(0, MODES)
        def _(to):
            @pl.when(to != mode)
            def _():
                slab(o, to, mode).wait_send()

    slabs_left(0)
    slabs_left(1)
    align_and_contract(3, (0, 1, 2, 3))

    column = jnp.sum(lines[...], axis=1, keepdims=True)
    lane = lax.broadcasted_iota(jnp.int32, (2 * OPS, 128), 1)
    tile = jnp.zeros((2 * OPS, 128), F32)
    for q in range(OPS):
        tile = jnp.where(lane == q, column[2 * OPS * q:2 * OPS * (q + 1)], tile)
    parts[mode] = tile

    @pl.loop(1, MODES)
    def _(step):
        remote(parts.at[mode], parts.at[mode], ps_send.at[step], ps_recv.at[step],
               (pair, (mode + step) % MODES)).start()

    slabs_left(2)
    slabs_left(3)

    @pl.loop(1, MODES)
    def _(step):
        remote(parts.at[mode], parts.at[mode], ps_send.at[step], ps_recv.at[step],
               (pair, (mode + step) % MODES)).wait()

    total = parts[0]
    for n in range(1, MODES):
        total = total + parts[n]
    total = total * (1.0 / order)
    for o in range(OPS):
        corr_ref[0, o] = total[2 * o:2 * o + 2, :OPS]


def body(time_pairs, slot_of, elementals, propagators):
    _, ops, parts, rows, order = elementals.shape
    slots = slot_of.shape[0]
    quarter = order // XS
    dma = pltpu.SemaphoreType.DMA
    sink, corr = pl.pallas_call(
        kernel,
        out_shape=(
            pltpu.VMEM(elementals.shape, BF16),
            pltpu.VMEM((1, ops, 2, ops), F32),
        ),
        in_specs=[
            pl.BlockSpec(memory_space=pl.ANY),
            pl.BlockSpec(memory_space=pl.ANY),
            pl.BlockSpec(memory_space=pl.ANY),
            pl.BlockSpec(memory_space=pl.ANY),
        ],
        out_specs=(pl.BlockSpec(memory_space=pltpu.VMEM), pl.BlockSpec(memory_space=pltpu.VMEM)),
        scratch_shapes=[
            *[pltpu.VMEM((slots, 2, rows, quarter), BF16)] * OPS,
            pltpu.VMEM((ops, 2, XS - 1, 2, rows, quarter), BF16),
            pltpu.VMEM((ops, 2, rows, order), BF16),
            pltpu.VMEM((ops, 2, rows, order), BF16),
            pltpu.VMEM((2, order, order), BF16),
            pltpu.VMEM((256, order), BF16),
            pltpu.VMEM((256, order), BF16),
            pltpu.VMEM((2 * rows, 2 * order), BF16),
            pltpu.VMEM((ops, MODES, rows // 2, 4 * rows), BF16),
            pltpu.VMEM((ops, MODES, rows // 2, 4 * rows), BF16),
            pltpu.VMEM((ops, 2, rows, order), BF16),
            pltpu.SMEM(time_pairs.shape, jnp.int32),
            pltpu.SMEM(slot_of.shape, jnp.int32),
            pltpu.VMEM((XS, 8, 128), jnp.int32),
            pltpu.SMEM((XS, 8, 128), jnp.int32),
            pltpu.VMEM((ops * ops * 2, 128), F32),
            pltpu.VMEM((MODES, 2 * ops, 128), F32),
            dma((XS - 1,)), dma((XS - 1,)),
            dma((OPS, XS - 1)), dma((OPS, XS - 1)),
            dma((OPS,)), dma((OPS,)),
            dma((OPS, 2, XS - 1)), dma((OPS, 2, XS - 1)),
            dma((24,)), dma((24,)),
            dma((OPS, MODES)), dma((OPS, MODES)),
            dma((MODES,)), dma((MODES,)),
            dma((3 + OPS + OPS,)),
        ],
        compiler_params=pltpu.CompilerParams(
            collective_id=0, has_side_effects=True, vmem_limit_bytes=56 << 20
        ),
        name="meson",
    )(time_pairs, slot_of, elementals, propagators)
    return jnp.swapaxes(corr, 2, 3), sink


def solution(mesh):
    in_specs = (
        P("pair", None),
        P(),
        P("pair", None, None, "mode", None),
        P("pair", None, "mode", None),
    )
    out_specs = (P("pair", None, None, None), P("pair", None, None, "mode", None))
    return jax.shard_map(body, mesh=mesh, in_specs=in_specs, out_specs=out_specs, check_vma=False)
```
